128 devices in a mesh: chan: 16 (over z, x_hi, core), rows: 8 (over x_lo, y).
Axes of the slice: x: 4 (x_hi: 2, x_lo: 2; x = x_hi * 2 + x_lo), y: 4, z: 4, core: 2. Of those that a mesh axis runs over, the one named last changes fastest.
Arguments:
- latents: bfloat16 [480, 6, 32, 512], P(None, None, 'rows', 'chan'), may hold values from -60 to 60
- conv_in_weight: bfloat16 [3, 3, 3, 512, 512], P(None, None, None, None, 'chan'), may hold values from -0.0546875 to 0.0546875
- conv_in_bias: float32 [512], replicated, may hold values from -4 to 4
- norm_gain: float32 [512], replicated, may hold values from 0.5 to 1.5
- norm_shift: float32 [512], replicated, may hold values from -3 to 3
- hidden_rim: bfloat16 [960, 2, 64, 512], P('chan', None, 'rows'), may hold values from -0.29882812 to 2
- conv_out_weight: bfloat16 [3, 3, 3, 512, 256], replicated, may hold values from -0.0546875 to 0.0546875
- conv_out_bias: float32 [256], replicated, may hold values from -3 to 3
Outputs:
- decoded: bfloat16 [960, 4, 64, 256], P('chan', None, 'rows')
The draws below stay inside these ranges and needn't reach their ends.
All inputs are finite; a program needn't handle non-finite values.
Results may differ from the reference program's by a relative error of at most 0.0042.
Values may be sent and summed in bfloat16 or wider, within the bound.
No kernel may reach another device: no remote copies, remote signals or barrier semaphores. Data moves between devices by JAX's collectives and lax.ppermute only.
A program may use at most 768 MiB of HBM per device.

```python
import jax
import jax.numpy as jnp
from jax import lax

C1 = 512
C2 = 256
GROUPS = 32
F = 4
W1 = 480
H1 = 32


def draw_latents(key, part):
    key = jax.random.fold_in(key, 7)
    sample_key, frame_key, sign_key, row_key, column_key = jax.random.split(key, 5)
    array_shape = (W1, F + 2, H1, C1)
    sample = jnp.clip(jax.random.normal(sample_key, array_shape, jnp.float32), -6.0, 6.0)
    heading = (2 * jax.random.randint(sign_key, (), 0, 2) - 1).astype(jnp.float32)
    frame_pos = jnp.arange(F + 2, dtype=jnp.float32) - 0.5 * (F + 1)
    frame_jitter = jax.random.uniform(frame_key, (F + 2,), jnp.float32, -0.05, 0.05)
    frame_exp = heading * frame_pos * (2.0 / (F + 1)) + frame_jitter
    row_exp = jax.random.uniform(row_key, (H1,), jnp.float32, -0.6, 0.6)
    column_exp = jax.random.uniform(column_key, (W1,), jnp.float32, -0.6, 0.6)
    scaling = jnp.exp(column_exp[:, None, None, None] + frame_exp[None, :, None, None] + row_exp[None, None, :, None])
    return (sample * scaling).astype(jnp.bfloat16)


def block_scale(key, dims, cuts, smallest, top_value):
    def one(dim, shards_of):
        heights = jax.random.uniform(jax.random.fold_in(jax.random.fold_in(key, 6), dim), (shards_of,), jnp.float32, smallest / len(cuts), top_value / len(cuts))
        return jnp.repeat(jnp.exp(heights), dims[dim] // shards_of).reshape((-1,) + (1,) * (len(dims) - dim - 1))

    loudness = one(*cuts[0])
    for cut in cuts[1:]:
        loudness = loudness * one(*cut)
    return loudness


def normal_values(own_key, extent, deviation, bound, pieces=(), kind=jnp.bfloat16):
    factor_of = block_scale(own_key, extent, pieces, -0.22, 0.18) if pieces else 1.0
    drawn = jax.random.normal(own_key, extent, jnp.float32) * deviation * factor_of
    return jnp.minimum(jnp.maximum(drawn, -bound), bound).astype(kind)


def setup_inputs(seed: int = 0) -> dict:
    splits = jax.random.split(jax.random.key(seed), 9)
    return {
        "latents": draw_latents(jax.random.fold_in(splits[8], 71), 0),
        "conv_in_weight": normal_values(splits[1], (3, 3, 3, C1, C1), (27 * C1) ** -0.5, 0.0546875, ((4, 16),)),
        "conv_in_bias": normal_values(splits[2], (C1,), 1.0, 4.0, (), jnp.float32),
        "norm_gain": jnp.clip(jax.random.uniform(splits[3], (C1,), jnp.float32, 0.5, 1.5), 0.5, 1.5),
        "norm_shift": normal_values(splits[4], (C1,), 0.5, 3.0, (), jnp.float32),
        "hidden_rim": jnp.clip(-0.29882812 + 2.2988281 * jax.random.uniform(splits[5], (2 * W1, 2, 2 * H1, C1), jnp.float32) ** block_scale(splits[5], (2 * W1, 2, 2 * H1, C1), ((0, 16), (2, 8)), -0.2, 0.2), -0.29882812, 2.0).astype(jnp.bfloat16),
        "conv_out_weight": normal_values(splits[6], (3, 3, 3, C1, C2), (27 * C1) ** -0.5, 0.0546875),
        "conv_out_bias": normal_values(splits[7], (C2,), 0.5, 3.0, (), jnp.float32),
    }


def conv_taps(padded, weight):
    columns = padded.shape[0] - 2
    frames = padded.shape[1] - 2
    height = padded.shape[2] - 2
    summed = jnp.zeros((columns, frames, height, weight.shape[4]), jnp.float32)
    for t_tap in range(3):
        for h_tap in range(3):
            for w_tap in range(3):
                window = padded[w_tap:w_tap + columns, t_tap:t_tap + frames, h_tap:h_tap + height].astype(jnp.float32)
                summed = summed + jnp.einsum('wthc,cd->wthd', window, weight[t_tap, h_tap, w_tap].astype(jnp.float32))
    return summed

def reference(latents, conv_in_weight, conv_in_bias, norm_gain, norm_shift, hidden_rim, conv_out_weight, conv_out_bias):
    padded = jnp.pad(latents, ((1, 1), (0, 0), (1, 1), (0, 0)))
    first = (conv_taps(padded, conv_in_weight) + conv_in_bias).astype(jnp.bfloat16)
    values = first.astype(jnp.float32)
    grouped = values.reshape(values.shape[:3] + (GROUPS, C1 // GROUPS))
    counted = float(values.size // GROUPS)
    mean = lax.optimization_barrier(jnp.sum(grouped, axis=(0, 1, 2, 4))) / counted
    var = lax.optimization_barrier(jnp.sum(grouped * grouped, axis=(0, 1, 2, 4))) / counted - mean * mean
    mean_chan = jnp.repeat(mean, C1 // GROUPS)
    inv_chan = jnp.repeat(1.0 / jnp.sqrt(var + 1e-06), C1 // GROUPS)
    normed = jax.nn.silu((values - mean_chan) * (inv_chan * norm_gain) + norm_shift).astype(jnp.bfloat16)
    upsampled = jnp.repeat(jnp.repeat(normed, 2, axis=0), 2, axis=2)
    stacked = jnp.concatenate([hidden_rim, upsampled], axis=1)
    padded_out = jnp.pad(stacked, ((1, 1), (0, 0), (1, 1), (0, 0)))
    return (conv_taps(padded_out, conv_out_weight) + conv_out_bias).astype(jnp.bfloat16)
```

```python
import jax
import jax.numpy as jnp
from jax import lax
from jax.experimental import pallas as pl
from jax.experimental.pallas import tpu as pltpu
from jax.sharding import PartitionSpec as P

GROUPS = 32
BOTH = ("chan", "rows")
BF16 = jnp.bfloat16
F32 = jnp.float32
VMEM = 58 * 1024 * 1024


def device_perm(move):
    pairs = []
    for d in range(128):
        chan, row = divmod(d, 8)
        to = move(chan // 4, chan // 2 % 2, chan % 2, row)
        if to is not None:
            z, half, core, row = to
            pairs.append((d, ((z % 4) * 4 + half * 2 + core) * 8 + row))
    return pairs


def send(array, move):
    return lax.ppermute(array, BOTH, device_perm(move))


def to_row(step):
    return lambda z, half, core, row: (z, half, core, row + step) if 0 <= row + step < 8 else None


def to_chan(step):
    def move(z, half, core, row):
        chan = z * 4 + half * 2 + core + step
        return (chan // 4, chan // 2 % 2, chan % 2, row) if 0 <= chan < 16 else None

    return move


def conv_in_kernel(place, main, other, up, up_other, down, down_other, w0, w1, w2, w3, bias,
                   strips, stats, x, w, turned, moments, sems):
    z, half, core = place[0], place[1], place[2]
    copies = []
    count = 0
    for array, slab, owner in (
        (main, slice(1, 5), core), (other, slice(1, 5), 1 - core),
        (up, 0, core), (up_other, 0, 1 - core), (down, 5, core), (down_other, 5, 1 - core),
    ):
        for k in range(8):
            dz, dh = k // 2, k % 2
            start = (((z + 4 - dz) % 4) * 4 + (half + dh) % 2 * 2 + owner) * 32
            copies.append(pltpu.make_async_copy(
                array.at[k], x.at[:, slab, pl.ds(pl.multiple_of(start, 32), 32), :], sems.at[count]))
            count += 1
    for dz, array in enumerate((w0, w1, w2, w3)):
        copies.append(pltpu.make_async_copy(array, w.at[:, :, (z + 4 - dz) % 4], sems.at[count]))
        count += 1
    for copy in copies:
        copy.start()
    moments[...] = jnp.zeros_like(moments)
    lane = lax.broadcasted_iota(jnp.int32, (128, 128), 1)
    inside = (lane >= 4) & (lane < 124)
    for copy in copies:
        copy.wait()

    def frame(t, _):
        for g in range(2):
            summed = None
            for a in range(3):
                for b in range(3):
                    rhs = jnp.concatenate([x[t + a, b + g * 2 + h] for h in range(2)], axis=1)
                    lhs = w[a * 3 + b].reshape(384, 512)
                    term = jnp.dot(lhs, rhs, preferred_element_type=F32)
                    summed = term if summed is None else summed + term
            for h in range(2):
                part = summed[:, h * 128 : (h + 1) * 128]
                value = pltpu.roll(part[0:128], 1, 1) + part[128:256] + pltpu.roll(part[256:384], 127, 1)
                value = (value + bias[...]).astype(BF16).astype(F32)
                kept = jnp.where(inside, value, 0.0)
                moments[0] += kept
                moments[1] += kept * kept
                turned[...] = value.T
                for s in range(4):
                    strips[s, t, g * 2 + h] = turned[3 + 30 * s : 35 + 30 * s, :].astype(BF16)
        return 0

    lax.fori_loop(0, 4, frame, 0)
    for i in range(2):
        grouped = jnp.sum(moments[i].reshape(8, 16, 128), axis=1)
        stats[i] = jnp.broadcast_to(jnp.sum(grouped, axis=1, keepdims=True), (8, 128))


def conv_in(place, main, other, up, up_other, down, down_other, weights, bias):
    return pl.pallas_call(
        conv_in_kernel,
        out_shape=(jax.ShapeDtypeStruct((4, 4, 4, 32, 128), BF16), jax.ShapeDtypeStruct((2, 8, 128), F32)),
        in_specs=[pl.BlockSpec(memory_space=pltpu.SMEM)] + [pl.BlockSpec(memory_space=pl.ANY)] * 10
        + [pl.BlockSpec(memory_space=pltpu.VMEM)],
        out_specs=(pl.BlockSpec(memory_space=pltpu.VMEM), pl.BlockSpec(memory_space=pltpu.VMEM)),
        scratch_shapes=[
            pltpu.VMEM((6, 6, 512, 128), BF16),
            pltpu.VMEM((9, 3, 4, 32, 512), BF16),
            pltpu.VMEM((128, 128), F32),
            pltpu.VMEM((2, 128, 128), F32),
            pltpu.SemaphoreType.DMA((52,)),
        ],
        compiler_params=pltpu.CompilerParams(vmem_limit_bytes=VMEM),
        cost_estimate=pl.CostEstimate(flops=7_200_000_000, bytes_accessed=9_000_000, transcendentals=0),
        name="conv_in",
    )(place, main, other, up, up_other, down, down_other, *weights, bias)


def collapse_kernel(taps, out):
    def pairs(t0, t1, t2):
        return ((t0, t1 + t2), (t0 + t1, t2))

    for z in range(4):
        wide = [[taps[0, b, c, z, 0].astype(F32) for c in range(3)] for b in range(3)]
        by_col = [pairs(*row) for row in wide]
        for pw in range(2):
            for i in range(2):
                by_row = pairs(by_col[0][pw][i], by_col[1][pw][i], by_col[2][pw][i])
                for ph in range(2):
                    for j in range(2):
                        out[0, ph, j, pw, i, 0, z] = by_row[ph][j].astype(BF16)


def collapse(weight):
    out = pl.pallas_call(
        collapse_kernel,
        grid=(3, 4),
        out_shape=jax.ShapeDtypeStruct((3, 2, 2, 2, 2, 4, 4, 32, 256), BF16),
        in_specs=[pl.BlockSpec((1, 3, 3, 4, 1, 32, 256), lambda a, p: (a, 0, 0, 0, p, 0, 0))],
        out_specs=pl.BlockSpec((1, 2, 2, 2, 2, 1, 4, 32, 256), lambda a, p: (a, 0, 0, 0, 0, p, 0, 0, 0)),
        compiler_params=pltpu.CompilerParams(vmem_limit_bytes=24 * 1024 * 1024),
        cost_estimate=pl.CostEstimate(flops=30_000_000, bytes_accessed=20_000_000, transcendentals=0),
        name="collapse",
    )(weight.reshape(3, 3, 3, 4, 4, 32, 256))
    return out.reshape(12, 2, 1024, 256)


def rim_kernel(rim, w, out):
    for pw in range(2):
        for t in range(2):
            summed = None
            for a in range(2 - t):
                for b in range(3):
                    lhs = rim[t + a, b : b + 8, :, pw * 512 : pw * 512 + 1536].reshape(256, 1536)
                    term = jnp.dot(lhs, w[a, b], preferred_element_type=F32)
                    summed = term if summed is None else summed + term
            summed = summed.reshape(8, 32, 256)
            for r in range(8):
                out[pw, r % 2, t, r // 2] = summed[r]


def conv_rim(windows, weight):
    return pl.pallas_call(
        rim_kernel,
        grid=(1,),
        out_shape=jax.ShapeDtypeStruct((2, 2, 2, 4, 32, 256), F32),
        in_specs=[
            pl.BlockSpec((2, 10, 32, 2048), lambda i: (0, 0, 0, 0)),
            pl.BlockSpec((2, 3, 1536, 256), lambda i: (0, 0, 0, 0)),
        ],
        out_specs=pl.BlockSpec((2, 2, 2, 4, 32, 256), lambda i: (0,) * 6),
        compiler_params=pltpu.CompilerParams(vmem_limit_bytes=40 * 1024 * 1024),
        cost_estimate=pl.CostEstimate(flops=3_600_000_000, bytes_accessed=9_500_000, transcendentals=0),
        name="conv_rim",
    )(windows, weight.reshape(3, 3, 1536, 256))


def conv_out_kernel(place, main, up, down, vectors, rim, bias, w, out, n, acc):
    step = pl.program_id(0)

    @pl.when(step == 0)
    def _():
        own, left, right, top, bottom = (place[i] for i in range(5))
        row = lax.broadcasted_iota(jnp.int32, (32, 128), 0)
        keep_col = jnp.where(
            ((row == 0) & (left == 1)) | ((row == 31) & (right == 1)), 0.0, 1.0)
        keep = [keep_col] * 6
        keep[0] = keep_col * jnp.where(top == 1, 0.0, 1.0)
        keep[5] = keep_col * jnp.where(bottom == 1, 0.0, 1.0)

        def frame(t, _):
            for r in range(4):
                p = own ^ r
                vec = vectors[p]
                for h in range(6):
                    raw = up[r, t] if h == 0 else down[r, t] if h == 5 else main[r, t, h - 1]
                    v = (raw.astype(F32) - vec[0:1]) * vec[1:2] + vec[2:3]
                    v = v / (1.0 + jnp.exp(-v)) * keep[h]
                    for s in range(3):
                        moved = v if s == 0 else pltpu.roll(v, 32 - s, 0)
                        start = pl.multiple_of(s * 512 + p * 128, 128)
                        n[t, h, :, pl.ds(start, 128)] = moved.astype(BF16)
            return 0

        lax.fori_loop(0, 4, frame, 0)
        whole = jnp.broadcast_to(bias[...], (32, 256))
        for pw in range(2):
            for ph in range(2):
                for t in range(4):
                    for h in range(4):
                        acc[pw, ph, t, h] = rim[pw, ph, t, h] + whole if t < 2 else whole

    a, ph, j = step // 4, step // 2 % 2, step % 2
    for tap in range(3):
        @pl.when(a == tap)
        def _():
            frames = 2 + tap
            for pw in range(2):
                lhs = n[0:frames, pl.ds(ph + j, 4), :, pw * 512 : pw * 512 + 1024].reshape(frames * 128, 1024)
                term = jnp.dot(lhs, w[0, pw], preferred_element_type=F32).reshape(frames, 4, 32, 256)
                acc[pw, ph, 4 - frames : 4] += term

    @pl.when(step == 11)
    def _():
        out[...] = acc[...].astype(BF16)


def conv_out(place, main, up, down, vectors, rim, bias, weight):
    whole = pl.BlockSpec(memory_space=pltpu.VMEM)
    return pl.pallas_call(
        conv_out_kernel,
        grid=(12,),
        out_shape=jax.ShapeDtypeStruct((2, 2, 4, 4, 32, 256), BF16),
        in_specs=[pl.BlockSpec(memory_space=pltpu.SMEM)] + [whole] * 6
        + [pl.BlockSpec((1, 2, 1024, 256), lambda i: (i, 0, 0, 0))],
        out_specs=pl.BlockSpec((2, 2, 4, 4, 32, 256), lambda i: (0,) * 6),
        scratch_shapes=[pltpu.VMEM((4, 6, 32, 1536), BF16), pltpu.VMEM((2, 2, 4, 4, 32, 256), F32)],
        compiler_params=pltpu.CompilerParams(vmem_limit_bytes=VMEM),
        cost_estimate=pl.CostEstimate(flops=4_900_000_000, bytes_accessed=18_000_000, transcendentals=400_000),
        name="conv_out",
    )(place, main, up, down, vectors, rim, bias, weight)


def rim_windows(rim):
    before, after = send(rim[59:60], to_chan(1)), send(rim[0:1], to_chan(-1))
    wide = jnp.concatenate([before, rim, after], axis=0)
    above, below = send(wide[:, :, 7:8], to_row(1)), send(wide[:, :, 0:1], to_row(-1))
    tall = jnp.concatenate([above, wide, below], axis=2)
    pairs = tall.transpose(1, 2, 0, 3).reshape(2, 10, 31, 1024)
    windows = jnp.concatenate([pairs[:, :, 0:30], pairs[:, :, 1:31]], axis=3)
    return jnp.pad(windows, ((0, 0), (0, 0), (0, 2), (0, 0)))


def body(
    latents,
    conv_in_weight,
    conv_in_bias,
    norm_gain,
    norm_shift,
    hidden_rim,
    conv_out_weight,
    conv_out_bias,
):
    chan, row = lax.axis_index("chan"), lax.axis_index("rows")
    z, half, core = chan // 4, chan // 2 % 2, chan % 2
    own = chan % 4
    flip_core = lambda z, half, core, row: (z, half, 1 - core, row)

    weights = conv_in_weight.swapaxes(3, 4)
    weight_of = [weights]
    for dz in range(1, 4):
        weight_of.append(send(weights, lambda z, half, core, row: (z + dz, half, core, row)))
    weight_of = [array.reshape(9, 3, 32, 512) for array in weight_of]

    padded = jnp.pad(latents.transpose(1, 2, 3, 0), ((0, 0), (0, 0), (0, 0), (4, 4)))
    pieces = jnp.stack([padded[..., 120 * i : 120 * i + 128] for i in range(4)])
    got = []
    for k in range(8):
        dz, dh = k // 2, k % 2
        piece = lax.dynamic_index_in_dim(pieces, (z + dz) % 4, 0, keepdims=False)
        if k:
            piece = send(piece, lambda z, half, core, row: (z + dz, half ^ dh, core, row))
        got.append(piece)
    main = jnp.stack(got)
    up, down = send(main[:, :, 3], to_row(1)), send(main[:, :, 0], to_row(-1))
    other, up_other, down_other = (send(array, flip_core) for array in (main, up, down))

    by_owner = conv_in_bias.reshape(4, 4, 32)
    bias = lax.dynamic_index_in_dim(by_owner, own, 1, keepdims=False).reshape(128, 1)
    place = jnp.stack([z, half, core]).astype(jnp.int32)
    strips, stats = conv_in(place, main, other, up, up_other, down, down_other, weight_of,
                            jnp.broadcast_to(bias, (128, 128)))

    parts = []
    for r in range(4):
        part = lax.dynamic_index_in_dim(strips, own ^ r, 0, keepdims=False)
        if r:
            part = send(part, lambda z, half, core, row: (z, half ^ (r // 2), core ^ (r % 2), row))
        parts.append(part)
    first = jnp.stack(parts)
    above, below = send(first[:, :, 3], to_row(1)), send(first[:, :, 0], to_row(-1))

    sent = jnp.broadcast_to(jnp.pad(stats[:, :, 0].reshape(1, 16), ((0, 0), (0, 112))), (128, 128))
    gathered = lax.all_to_all(sent, BOTH, split_axis=0, concat_axis=0, tiled=True)
    sums, squares = gathered.reshape(4, 4, 8, 128)[..., :16].sum(axis=(0, 2)).reshape(4, 2, 8).swapaxes(0, 1)
    counted = float(480 * 4 * 32 * 16)
    mean = sums / counted
    var = squares / counted - mean * mean
    inv = 1.0 / jnp.sqrt(var + 1e-06)
    by_place = lambda vector: vector.reshape(4, 4, 32).swapaxes(0, 1).reshape(4, 128)
    vectors = jnp.stack(
        [jnp.repeat(mean, 16, axis=1), jnp.repeat(inv, 16, axis=1) * by_place(norm_gain), by_place(norm_shift)]
        + [jnp.zeros((4, 128), F32)] * 5, axis=1)

    rim = conv_rim(rim_windows(hidden_rim), conv_out_weight)
    edges = jnp.stack([own, chan == 0, chan == 15, row == 0, row == 7]).astype(jnp.int32)
    decoded = conv_out(edges, first, above, below, vectors, rim, conv_out_bias.reshape(1, 256),
                       collapse(conv_out_weight))
    return decoded.transpose(4, 0, 2, 3, 1, 5)[:30].reshape(60, 4, 8, 256)


def solution(mesh):
    return jax.shard_map(
        body,
        mesh=mesh,
        in_specs=(
            P(None, None, "rows", "chan"),
            P(None, None, None, None, "chan"),
            P(),
            P(),
            P(),
            P("chan", None, "rows", None),
            P(),
            P(),
        ),
        out_specs=P("chan", None, "rows", None),
        check_vma=False,
    )
```

```python
import jax
import jax.numpy as jnp
from jax import lax
from jax.experimental import pallas as pl
from jax.experimental.pallas import tpu as pltpu
from jax.sharding import PartitionSpec as P

GROUPS = 32
BOTH = ("chan", "rows")
BF16 = jnp.bfloat16
F32 = jnp.float32


def device_perm(move):
    pairs = []
    for d in range(128):
        chan, row = divmod(d, 8)
        to = move(chan // 4, chan // 2 % 2, chan % 2, row)
        if to is not None:
            z, half, core, row = to
            pairs.append((d, ((z % 4) * 4 + half * 2 + core) * 8 + row))
    return pairs


def send(array, move):
    return lax.ppermute(array, BOTH, device_perm(move))


def to_row(step):
    return lambda z, half, core, row: (z, half, core, row + step) if 0 <= row + step < 8 else None


def to_chan(step):
    def move(z, half, core, row):
        chan = z * 4 + half * 2 + core + step
        return (chan // 4, chan // 2 % 2, chan % 2, row) if 0 <= chan < 16 else None

    return move


def conv_in_kernel(place, own, other, own_swap, other_swap, w0, w1, w3, near, far, bias,
                   strips, stats, x, w, turned, moments, sems):
    z, half, core, odd = (place[i] for i in range(4))

    def fetch(i, source, target):
        return pltpu.make_async_copy(source, target, sems.at[i])

    early, late = [], []
    for source, dh, owner in ((own, 0, core), (other, 1, core), (own_swap, 0, 1 - core), (other_swap, 1, 1 - core)):
        for dz in range(4):
            start = (((z + 4 - dz) % 4) * 4 + (half + dh) % 2 * 2 + owner) * 32
            rows = pl.ds(pl.multiple_of(start, 32), 32)
            for group, frames in ((early, pl.ds(0, 3)), (late, pl.ds(3, 3))):
                group.append((source.at[dz, :, frames], x.at[:, frames, rows, :]))
    for dz, source in ((0, w0), (1, w1), (3, w3)):
        early.append((source, w.at[:, :, (z + 4 - dz) % 4]))
    for which, source in ((odd, near), (1 - odd, far)):
        columns = pl.ds(pl.multiple_of(which * 256, 256), 256)
        early.append((source, w.at[:, :, (z + 2) % 4, :, columns]))
    early = [fetch(i, *pair) for i, pair in enumerate(early)]
    late = [fetch(i + len(early), *pair) for i, pair in enumerate(late)]
    for copy in early + late:
        copy.start()
    moments[...] = jnp.zeros_like(moments)
    lane = lax.broadcasted_iota(jnp.int32, (128, 128), 1)
    inside = (lane >= 4) & (lane < 124)

    def frame(t, _):
        for g in range(2):
            summed = None
            for a in range(3):
                for b in range(3):
                    rhs = jnp.concatenate([x[b + g * 2 + h, t + a] for h in range(2)], axis=1)
                    lhs = w[a * 3 + b].reshape(384, 512)
                    term = jnp.dot(lhs, rhs, preferred_element_type=F32)
                    summed = term if summed is None else summed + term
            for h in range(2):
                part = summed[:, h * 128 : (h + 1) * 128]
                value = pltpu.roll(part[0:128], 1, 1) + part[128:256] + pltpu.roll(part[256:384], 127, 1)
                value = (value + bias[...]).astype(BF16).astype(F32)
                kept = jnp.where(inside, value, 0.0)
                moments[0] += kept
                moments[1] += kept * kept
                turned[...] = value.T
                for s in range(4):
                    strips[s, t, g * 2 + h] = turned[3 + 30 * s : 35 + 30 * s, :].astype(BF16)
        return 0

    for copy in early:
        copy.wait()
    frame(0, 0)
    for copy in late:
        copy.wait()
    lax.fori_loop(1, 4, frame, 0)
    for i in range(2):
        grouped = jnp.sum(moments[i].reshape(8, 16, 128), axis=1)
        stats[i] = jnp.broadcast_to(jnp.sum(grouped, axis=1, keepdims=True), (8, 128))


def conv_in(place, parts, weights, bias):
    return pl.pallas_call(
        conv_in_kernel,
        out_shape=(jax.ShapeDtypeStruct((4, 4, 4, 32, 128), BF16), jax.ShapeDtypeStruct((2, 8, 128), F32)),
        in_specs=[pl.BlockSpec(memory_space=pltpu.SMEM)] + [pl.BlockSpec(memory_space=pl.ANY)] * 9
        + [pl.BlockSpec(memory_space=pltpu.VMEM)],
        out_specs=(pl.BlockSpec(memory_space=pltpu.VMEM), pl.BlockSpec(memory_space=pltpu.VMEM)),
        scratch_shapes=[
            pltpu.VMEM((6, 6, 512, 128), BF16),
            pltpu.VMEM((9, 3, 4, 32, 512), BF16),
            pltpu.VMEM((128, 128), F32),
            pltpu.VMEM((2, 128, 128), F32),
            pltpu.SemaphoreType.DMA((37,)),
        ],
        compiler_params=pltpu.CompilerParams(vmem_limit_bytes=24 * 1024 * 1024),
        cost_estimate=pl.CostEstimate(flops=7_200_000_000, bytes_accessed=9_000_000, transcendentals=0),
        name="conv_in",
    )(place, *parts, *weights, bias)


def collapse_kernel(taps, out):
    def pairs(t0, t1, t2):
        return ((t0, t1 + t2), (t0 + t1, t2))

    for z in range(4):
        wide = [[taps[0, b, c, z, 0].astype(F32) for c in range(3)] for b in range(3)]
        by_col = [pairs(*row) for row in wide]
        for pw in range(2):
            for i in range(2):
                by_row = pairs(by_col[0][pw][i], by_col[1][pw][i], by_col[2][pw][i])
                for ph in range(2):
                    for j in range(2):
                        out[0, ph, j, pw, i, 0, z] = by_row[ph][j].astype(BF16)


def collapse(weight):
    def kernel(taps, out):
        pltpu.emit_pipeline(
            collapse_kernel,
            grid=(3, 4),
            in_specs=[pl.BlockSpec((1, 3, 3, 4, 1, 32, 256), lambda a, p: (a, 0, 0, 0, p, 0, 0))],
            out_specs=[pl.BlockSpec((1, 2, 2, 2, 2, 1, 4, 32, 256), lambda a, p: (a, 0, 0, 0, 0, p, 0, 0, 0))],
        )(taps, out)

    out = pl.pallas_call(
        kernel,
        out_shape=jax.ShapeDtypeStruct((3, 2, 2, 2, 2, 4, 4, 32, 256), BF16),
        in_specs=[pl.BlockSpec(memory_space=pltpu.HBM)],
        out_specs=pl.BlockSpec(memory_space=pltpu.HBM),
        compiler_params=pltpu.CompilerParams(vmem_limit_bytes=50 * 1024 * 1024),
        cost_estimate=pl.CostEstimate(flops=0, bytes_accessed=0, transcendentals=0),
        name="collapse",
    )(weight.reshape(3, 3, 3, 4, 4, 32, 256))
    return out.reshape(12, 2, 1024, 256)


def rim_kernel(rim, weight, out, w, wide, fine, sem):
    fetch = pltpu.make_async_copy(weight.at[0:2], w, sem)
    fetch.start()
    for t in range(2):
        for h in range(10):
            line = rim[t, h].astype(F32)
            for s in range(3):
                moved = line if s == 0 else pltpu.roll(line, 64 - s, 0)
                wide[t, h, :, s * 512 : s * 512 + 512] = moved.astype(BF16)
    fetch.wait()
    for t in range(2):
        summed = None
        for a in range(2 - t):
            for b in range(3):
                lhs = wide[t + a, b : b + 8].reshape(512, 1536)
                term = jnp.dot(lhs, w[a, b], preferred_element_type=F32)
                summed = term if summed is None else summed + term
        for c in range(2):
            fine[...] = summed[:, c * 128 : c * 128 + 128].reshape(8, 64, 128)
            for r in range(8):
                for pw in range(2):
                    out[pw, r % 2, t, r // 2, :, c * 128 : c * 128 + 128] = fine[r, pl.ds(pw, 32, stride=2), :]


def conv_rim(tall, weight):
    return pl.pallas_call(
        rim_kernel,
        out_shape=jax.ShapeDtypeStruct((2, 2, 2, 4, 32, 256), F32),
        in_specs=[pl.BlockSpec(memory_space=pltpu.VMEM), pl.BlockSpec(memory_space=pltpu.HBM)],
        out_specs=pl.BlockSpec(memory_space=pltpu.VMEM),
        scratch_shapes=[
            pltpu.VMEM((2, 3, 1536, 256), BF16),
            pltpu.VMEM((2, 10, 64, 1536), BF16),
            pltpu.VMEM((8, 64, 128), F32),
            pltpu.SemaphoreType.DMA,
        ],
        compiler_params=pltpu.CompilerParams(vmem_limit_bytes=50 * 1024 * 1024),
        cost_estimate=pl.CostEstimate(flops=0, bytes_accessed=0, transcendentals=0),
        name="conv_rim",
    )(tall, weight.reshape(3, 3, 1536, 256))


def conv_out_kernel(place, main, up, down, vectors, rim, bias, weight, out, n, acc, w, sems):
    fetches = [pltpu.make_async_copy(weight.at[tap], w.at[tap], sems.at[tap]) for tap in range(3)]
    for fetch in fetches:
        fetch.start()
    own, left, right, top, bottom = (place[i] for i in range(5))
    row = lax.broadcasted_iota(jnp.int32, (32, 128), 0)
    keep_col = jnp.where(
        ((row == 0) & (left == 1)) | ((row == 31) & (right == 1)), 0.0, 1.0)
    keep = [keep_col] * 6
    keep[0] = keep_col * jnp.where(top == 1, 0.0, 1.0)
    keep[5] = keep_col * jnp.where(bottom == 1, 0.0, 1.0)

    def frame(t, _):
        for r in range(4):
            p = own ^ r
            vec = vectors[p]
            for h in range(6):
                raw = up[r, t] if h == 0 else down[r, t] if h == 5 else main[r, t, h - 1]
                v = (raw.astype(F32) - vec[0:1]) * vec[1:2] + vec[2:3]
                v = v / (1.0 + jnp.exp(-v)) * keep[h]
                for s in range(3):
                    moved = v if s == 0 else pltpu.roll(v, 32 - s, 0)
                    start = pl.multiple_of(s * 512 + p * 128, 128)
                    n[t, h, :, pl.ds(start, 128)] = moved.astype(BF16)
        return 0

    lax.fori_loop(0, 4, frame, 0)
    whole = jnp.broadcast_to(bias[...], (32, 256))
    for pw in range(2):
        for ph in range(2):
            for t in range(4):
                for h in range(4):
                    acc[pw, ph, t, h] = rim[pw, ph, t, h] + whole if t < 2 else whole

    for tap in range(3):
        fetches[tap].wait()
        frames = 2 + tap
        for ph in range(2):
            for j in range(2):
                for pw in range(2):
                    lhs = n[0:frames, ph + j : ph + j + 4, :, pw * 512 : pw * 512 + 1024]
                    term = jnp.dot(lhs.reshape(frames * 128, 1024), w[tap, ph * 2 + j, pw],
                                   preferred_element_type=F32)
                    acc[pw, ph, 4 - frames : 4] += term.reshape(frames, 4, 32, 256)
    out[...] = acc[...].astype(BF16)


def conv_out(place, main, up, down, vectors, rim, bias, weight):
    whole = pl.BlockSpec(memory_space=pltpu.VMEM)
    return pl.pallas_call(
        conv_out_kernel,
        out_shape=jax.ShapeDtypeStruct((2, 2, 4, 4, 32, 256), BF16),
        in_specs=[pl.BlockSpec(memory_space=pltpu.SMEM)] + [whole] * 6 + [pl.BlockSpec(memory_space=pltpu.HBM)],
        out_specs=whole,
        scratch_shapes=[
            pltpu.VMEM((4, 6, 32, 1536), BF16),
            pltpu.VMEM((2, 2, 4, 4, 32, 256), F32),
            pltpu.VMEM((3, 4, 2, 1024, 256), BF16),
            pltpu.SemaphoreType.DMA((3,)),
        ],
        compiler_params=pltpu.CompilerParams(vmem_limit_bytes=52 * 1024 * 1024),
        cost_estimate=pl.CostEstimate(flops=4_900_000_000, bytes_accessed=18_000_000, transcendentals=400_000),
        name="conv_out",
    )(place, main, up, down, vectors, rim, bias, weight.reshape(3, 4, 2, 1024, 256))


def body(
    latents,
    conv_in_weight,
    conv_in_bias,
    norm_gain,
    norm_shift,
    hidden_rim,
    conv_out_weight,
    conv_out_bias,
):
    chan, row = lax.axis_index("chan"), lax.axis_index("rows")
    z, half, core = chan // 4, chan // 2 % 2, chan % 2
    strip = chan % 4
    flip_core = lambda z, half, core, row: (z, half, 1 - core, row)

    flip_half = lambda z, half, core, row: (z, 1 - half, core, row)
    along_z = lambda dz: lambda z, half, core, row: (z + dz, half, core, row)

    weights = conv_in_weight.swapaxes(3, 4).reshape(9, 3, 32, 512)
    padded = jnp.pad(latents.transpose(2, 1, 3, 0), ((0, 0), (0, 0), (0, 0), (4, 28)))
    from_edge = lambda i, j: jnp.concatenate([padded[i].reshape(192, 512), hidden_rim[:, :, j].reshape(120, 512)])
    above, below = send(from_edge(3, 7), to_row(1)), send(from_edge(0, 0), to_row(-1))
    tall = jnp.concatenate([above[:192].reshape(1, 6, 32, 512), padded, below[:192].reshape(1, 6, 32, 512)])
    rim = jnp.concatenate([above[192:].reshape(60, 2, 1, 512), hidden_rim, below[192:].reshape(60, 2, 1, 512)], axis=2)

    pieces = jnp.stack([tall[..., 120 * i : 120 * i + 128] for i in range(4)])
    own = []
    for dz in range(4):
        piece = lax.dynamic_index_in_dim(pieces, (z + dz) % 4, 0, keepdims=False)
        own.append(send(piece, along_z(dz)) if dz else piece)
    own = jnp.stack(own)
    before, after = send(rim[59:60], to_chan(1)), send(rim[0:1], to_chan(-1))
    rim = jnp.concatenate([before, rim, after, jnp.zeros((2, 2, 10, 512), BF16)], axis=0).transpose(1, 2, 0, 3)

    own, rim, weights, conv_out_weight = lax.optimization_barrier((own, rim, weights, conv_out_weight))
    other = send(own, flip_half)
    odd = row % 2
    near = send(lax.dynamic_slice_in_dim(weights, odd * 256, 256, axis=3), along_z(2))
    own_swap = send(own, flip_core)
    collapsed = collapse(conv_out_weight)
    near_first, rim, collapsed = lax.optimization_barrier((near, rim, collapsed))
    far = send(near_first, lambda z, half, core, row: (z, half, core, row ^ 1))
    rim = conv_rim(rim, conv_out_weight)
    weights = [weights, send(weights, along_z(1)), send(weights, along_z(3)), near_first, far]
    other, collapsed, rim, weights = lax.optimization_barrier((other, collapsed, rim, weights))
    parts = [own, other, own_swap, send(other, flip_core)]

    by_owner = conv_in_bias.reshape(4, 4, 32)
    bias = lax.dynamic_index_in_dim(by_owner, strip, 1, keepdims=False).reshape(128, 1)
    place = jnp.stack([z, half, core, odd]).astype(jnp.int32)
    strips, stats = conv_in(place, parts, weights, jnp.broadcast_to(bias, (128, 128)))

    parts = []
    for r in range(4):
        part = lax.dynamic_index_in_dim(strips, strip ^ r, 0, keepdims=False)
        if r:
            part = send(part, lambda z, half, core, row: (z, half ^ (r // 2), core ^ (r % 2), row))
        parts.append(part)
    stats, parts[1] = lax.optimization_barrier((stats, parts[1]))
    sent = jnp.broadcast_to(jnp.pad(stats[:, :, 0].reshape(1, 16), ((0, 0), (0, 112))), (128, 128))
    first = jnp.stack(parts)
    above, below = send(first[:, :, 3], to_row(1)), send(first[:, :, 0], to_row(-1))
    gathered = lax.all_to_all(sent, BOTH, split_axis=0, concat_axis=0, tiled=True)
    sums, squares = gathered.reshape(4, 4, 8, 128)[..., :16].sum(axis=(0, 2)).reshape(4, 2, 8).swapaxes(0, 1)
    counted = float(480 * 4 * 32 * 16)
    mean = sums / counted
    var = squares / counted - mean * mean
    inv = 1.0 / jnp.sqrt(var + 1e-06)
    by_place = lambda vector: vector.reshape(4, 4, 32).swapaxes(0, 1).reshape(4, 128)
    vectors = jnp.stack(
        [jnp.repeat(mean, 16, axis=1), jnp.repeat(inv, 16, axis=1) * by_place(norm_gain), by_place(norm_shift)]
        + [jnp.zeros((4, 128), F32)] * 5, axis=1)

    edges = jnp.stack([strip, chan == 0, chan == 15, row == 0, row == 7]).astype(jnp.int32)
    decoded = conv_out(edges, first, above, below, vectors, rim, conv_out_bias.reshape(1, 256),
                       collapsed)
    return decoded.transpose(4, 0, 2, 3, 1, 5)[:30].reshape(60, 4, 8, 256)


def solution(mesh):
    return jax.shard_map(
        body,
        mesh=mesh,
        in_specs=(
            P(None, None, "rows", "chan"),
            P(None, None, None, None, "chan"),
            P(),
            P(),
            P(),
            P("chan", None, "rows", None),
            P(),
            P(),
        ),
        out_specs=P("chan", None, "rows", None),
        check_vma=False,
    )
```

```python
import jax
import jax.numpy as jnp
from jax import lax
from jax.experimental import pallas as pl
from jax.experimental.pallas import tpu as pltpu
from jax.sharding import PartitionSpec as P

GROUPS = 32
BOTH = ("chan", "rows")
BF16 = jnp.bfloat16
F32 = jnp.float32


def device_perm(move):
    pairs = []
    for d in range(128):
        chan, row = divmod(d, 8)
        to = move(chan // 4, chan // 2 % 2, chan % 2, row)
        if to is not None:
            z, half, core, row = to
            pairs.append((d, ((z % 4) * 4 + half * 2 + core) * 8 + row))
    return pairs


def send(array, move):
    return lax.ppermute(array, BOTH, device_perm(move))


def to_row(step):
    return lambda z, half, core, row: (z, half, core, row + step) if 0 <= row + step < 8 else None


def to_chan(step):
    def move(z, half, core, row):
        chan = z * 4 + half * 2 + core + step
        return (chan // 4, chan // 2 % 2, chan % 2, row) if 0 <= chan < 16 else None

    return move


def conv_in_kernel(place, own, other, own_swap, other_swap, own_edge, other_edge, own_edge_swap, other_edge_swap,
                   w0, w1, w3, near, far, bias, strip0, strip1, strip2, strip3, stats,
                   x, w, acc, turned, moments, sems):
    z, half, core, odd = (place[i] for i in range(4))

    def fetch(i, source, target):
        return pltpu.make_async_copy(source, target, sems.at[i])

    groups = []
    for tap, frames in ((0, pl.ds(0, 1)), (1, pl.ds(1, 1)), (2, pl.ds(2, 1)), (None, pl.ds(3, 3))):
        group = []
        for source, ends, dh, owner in (
            (own, own_edge, 0, core), (other, other_edge, 1, core),
            (own_swap, own_edge_swap, 0, 1 - core), (other_swap, other_edge_swap, 1, 1 - core),
        ):
            block = (half + dh) % 2 * 2 + owner
            group.append((source.at[:, :, frames], x.at[:, 1:5, frames, block]))
            for side in range(2):
                group.append((ends.at[:, side, frames], x.at[:, 5 * side, frames, block]))
        if tap is not None:
            taps = pl.ds(3 * tap, 3)
            for dz, source in ((0, w0), (1, w1), (3, w3)):
                group.append((source.at[taps], w.at[taps, :, (z + 4 - dz) % 4]))
            for which, source in ((odd, near), (1 - odd, far)):
                columns = pl.ds(pl.multiple_of(which * 256, 256), 256)
                group.append((source.at[taps], w.at[taps, :, (z + 2) % 4, :, columns]))
        start = sum(len(g) for g in groups)
        groups.append([fetch(start + i, *pair) for i, pair in enumerate(group)])
    for group in groups:
        for copy in group:
            copy.start()
    moments[...] = jnp.zeros_like(moments)
    lane = lax.broadcasted_iota(jnp.int32, (128, 128), 1)
    inside = (lane >= 4) & (lane < 124)

    def frame_tap(t, g, a):
        summed = None
        for b in range(3):
            rhs = jnp.concatenate([x[:, b + g * 2 + h, t + a].reshape(512, 128) for h in range(2)], axis=1)
            lhs = w[a * 3 + b].reshape(384, 512)
            term = jnp.dot(lhs, rhs, preferred_element_type=F32)
            summed = term if summed is None else summed + term
        return summed

    def finish(t, g, summed):
        for h in range(2):
            part = summed[:, h * 128 : (h + 1) * 128]
            value = pltpu.roll(part[0:128], 1, 1) + part[128:256] + pltpu.roll(part[256:384], 127, 1)
            value = (value + bias[...]).astype(BF16).astype(F32)
            kept = jnp.where(inside, value, 0.0)
            moments[0] += kept
            moments[1] += kept * kept
            turned[...] = value.T
            for r, strip in enumerate((strip0, strip1, strip2, strip3)):
                strip[g * 2 + h, t] = turned[pl.ds(3 + 30 * ((half * 2 + core) ^ r), 32), :].astype(BF16)

    def frame(t, _):
        for g in range(2):
            finish(t, g, frame_tap(t, g, 0) + frame_tap(t, g, 1) + frame_tap(t, g, 2))
        return 0

    for a in range(3):
        for copy in groups[a]:
            copy.wait()
        for g in range(2):
            term = frame_tap(0, g, a)
            if a == 0:
                acc[g] = term
            elif a == 1:
                acc[g] += term
            else:
                finish(0, g, acc[g] + term)
    for copy in groups[3]:
        copy.wait()
    lax.fori_loop(1, 4, frame, 0)
    lane, group = (lax.broadcasted_iota(jnp.int32, (8, 128), i) for i in (1, 0))
    row = jnp.zeros((1, 128), F32)
    for i in range(2):
        grouped = jnp.sum(moments[i].reshape(8, 16, 128), axis=1)
        totals = jnp.sum(grouped, axis=1, keepdims=True)
        row += jnp.sum(jnp.where(lane == group + 8 * i, totals, 0.0), axis=0, keepdims=True)
    stats[...] = jnp.broadcast_to(row, (128, 128))


def conv_in(place, parts, weights, bias):
    return pl.pallas_call(
        conv_in_kernel,
        out_shape=[jax.ShapeDtypeStruct((4, 4, 32, 128), BF16)] * 4 + [jax.ShapeDtypeStruct((128, 128), F32)],
        in_specs=[pl.BlockSpec(memory_space=pltpu.SMEM)] + [pl.BlockSpec(memory_space=pl.ANY)] * 13
        + [pl.BlockSpec(memory_space=pltpu.VMEM)],
        out_specs=[pl.BlockSpec(memory_space=pltpu.VMEM)] * 5,
        scratch_shapes=[
            pltpu.VMEM((4, 6, 6, 4, 32, 128), BF16),
            pltpu.VMEM((9, 3, 4, 32, 512), BF16),
            pltpu.VMEM((2, 384, 256), F32),
            pltpu.VMEM((128, 128), F32),
            pltpu.VMEM((2, 128, 128), F32),
            pltpu.SemaphoreType.DMA((63,)),
        ],
        compiler_params=pltpu.CompilerParams(vmem_limit_bytes=56 * 1024 * 1024),
        cost_estimate=pl.CostEstimate(flops=7_200_000_000, bytes_accessed=9_000_000, transcendentals=0),
        name="conv_in",
    )(place, *parts, *weights, bias)


def collapse(taps, out):
    def pairs(t0, t1, t2):
        return ((t0, t1 + t2), (t0 + t1, t2))

    for z in range(4):
        for p in range(4):
            source = z * 128 + p * 32
            target = p * 128 + z * 32
            wide = [[taps[b, c, source : source + 32, :].astype(F32) for c in range(3)] for b in range(3)]
            by_col = [pairs(*row) for row in wide]
            for pw in range(2):
                for side in range(2):
                    by_row = pairs(by_col[0][pw][side], by_col[1][pw][side], by_col[2][pw][side])
                    for ph in range(2):
                        for j in range(2):
                            out[ph, j, pw, side * 512 + target : side * 512 + target + 32, :] = by_row[ph][j].astype(BF16)


def rim_kernel(rim, above, below, before, after, weight, out, w, wide, fine, sem):
    fetch = pltpu.make_async_copy(weight.at[0:2], w, sem)
    fetch.start()
    column = lax.broadcasted_iota(jnp.int32, (64, 512), 0)
    for t in range(2):
        for h in range(10):
            line = above[t] if h == 0 else below[t] if h == 9 else rim[t, h - 1]
            line = pltpu.roll(line.astype(F32), 1, 0)
            line = jnp.where(column == 0, before[t, h : h + 1].astype(F32), line)
            line = jnp.where(column == 61, after[t, h : h + 1].astype(F32), line)
            for s in range(3):
                moved = line if s == 0 else pltpu.roll(line, 64 - s, 0)
                wide[t, h, :, s * 512 : s * 512 + 512] = moved.astype(BF16)
    fetch.wait()
    for t in range(2):
        summed = None
        for a in range(2 - t):
            for b in range(3):
                lhs = wide[t + a, b : b + 8].reshape(512, 1536)
                term = jnp.dot(lhs, w[a, b], preferred_element_type=F32)
                summed = term if summed is None else summed + term
        for c in range(2):
            fine[...] = summed[:, c * 128 : c * 128 + 128].reshape(8, 64, 128)
            for r in range(8):
                for pw in range(2):
                    out[pw, r % 2, t, r // 2, :, c * 128 : c * 128 + 128] = fine[r, pl.ds(pw, 32, stride=2), :]


def conv_rim(rim, above, below, before, after, weight):
    return pl.pallas_call(
        rim_kernel,
        out_shape=jax.ShapeDtypeStruct((2, 2, 2, 4, 32, 256), F32),
        in_specs=[pl.BlockSpec(memory_space=pltpu.VMEM)] * 5 + [pl.BlockSpec(memory_space=pltpu.HBM)],
        out_specs=pl.BlockSpec(memory_space=pltpu.VMEM),
        scratch_shapes=[
            pltpu.VMEM((2, 3, 1536, 256), BF16),
            pltpu.VMEM((2, 10, 64, 1536), BF16),
            pltpu.VMEM((8, 64, 128), F32),
            pltpu.SemaphoreType.DMA,
        ],
        compiler_params=pltpu.CompilerParams(vmem_limit_bytes=50 * 1024 * 1024),
        cost_estimate=pl.CostEstimate(flops=0, bytes_accessed=0, transcendentals=0),
        name="conv_rim",
    )(rim, above, below, before, after, weight.reshape(3, 3, 1536, 256))


def conv_out_kernel(place, main, up, down, vectors, rim, bias, weight, out, n, acc, raw, w0, w1, w2, sems):
    fetches = [pltpu.make_async_copy(weight.at[tap], raw.at[tap], sems.at[tap]) for tap in range(3)]
    for fetch in fetches:
        fetch.start()
    own, left, right, top, bottom = (place[i] for i in range(5))
    row = lax.broadcasted_iota(jnp.int32, (32, 128), 0)
    keep_col = jnp.where(
        ((row == 0) & (left == 1)) | ((row == 31) & (right == 1)), 0.0, 1.0)
    keep = [keep_col] * 6
    keep[0] = keep_col * jnp.where(top == 1, 0.0, 1.0)
    keep[5] = keep_col * jnp.where(bottom == 1, 0.0, 1.0)

    def frame(t, _):
        for r in range(4):
            p = own ^ r
            vec = vectors[p]
            for h in range(6):
                raw = up[r, t] if h == 0 else down[r, t] if h == 5 else main[r, h - 1, t]
                v = (raw.astype(F32) - vec[0:1]) * vec[1:2] + vec[2:3]
                v = v / (1.0 + jnp.exp(-v)) * keep[h]
                for s in range(3):
                    moved = v if s == 0 else pltpu.roll(v, 32 - s, 0)
                    start = pl.multiple_of(s * 512 + p * 128, 128)
                    n[t, h, :, pl.ds(start, 128)] = moved.astype(BF16)
        return 0

    lax.fori_loop(0, 4, frame, 0)
    whole = jnp.broadcast_to(bias[...], (32, 256))
    for pw in range(2):
        for ph in range(2):
            for t in range(4):
                for h in range(4):
                    acc[pw, ph, t, h] = rim[pw, ph, t, h] + whole if t < 2 else whole

    def multiply(tap, w):
        frames = 2 + tap
        for ph in range(2):
            for j in range(2):
                for pw in range(2):
                    lhs = n[0:frames, ph + j : ph + j + 4, :, pw * 512 : pw * 512 + 1024]
                    term = jnp.dot(lhs.reshape(frames * 128, 1024), w[ph, j, pw], preferred_element_type=F32)
                    acc[pw, ph, 4 - frames : 4] += term.reshape(frames, 4, 32, 256)

    for fetch in fetches:
        fetch.wait()
    collapse(raw.at[2], w2)
    multiply(2, w2)
    collapse(raw.at[1], w1)
    multiply(1, w1)
    collapse(raw.at[0], w0)
    multiply(0, w0)
    out[...] = acc[...].astype(BF16)


def conv_out(place, main, up, down, vectors, rim, bias, weight):
    whole = pl.BlockSpec(memory_space=pltpu.VMEM)
    return pl.pallas_call(
        conv_out_kernel,
        out_shape=jax.ShapeDtypeStruct((2, 2, 4, 4, 32, 256), BF16),
        in_specs=[pl.BlockSpec(memory_space=pltpu.SMEM)] + [whole] * 6 + [pl.BlockSpec(memory_space=pltpu.HBM)],
        out_specs=whole,
        scratch_shapes=[
            pltpu.VMEM((4, 6, 32, 1536), BF16),
            pltpu.VMEM((2, 2, 4, 4, 32, 256), F32),
            pltpu.VMEM((3, 3, 3, 512, 256), BF16),
            pltpu.VMEM((2, 2, 2, 1024, 256), BF16),
            pltpu.VMEM((2, 2, 2, 1024, 256), BF16),
            pltpu.VMEM((2, 2, 2, 1024, 256), BF16),
            pltpu.SemaphoreType.DMA((3,)),
        ],
        compiler_params=pltpu.CompilerParams(vmem_limit_bytes=52 * 1024 * 1024),
        cost_estimate=pl.CostEstimate(flops=4_900_000_000, bytes_accessed=18_000_000, transcendentals=400_000),
        name="conv_out",
    )(place, main, up, down, vectors, rim, bias, weight)


def body(
    latents,
    conv_in_weight,
    conv_in_bias,
    norm_gain,
    norm_shift,
    hidden_rim,
    conv_out_weight,
    conv_out_bias,
):
    chan, row = lax.axis_index("chan"), lax.axis_index("rows")
    z, half, core = chan // 4, chan // 2 % 2, chan % 2
    strip = chan % 4
    flip_core = lambda z, half, core, row: (z, half, 1 - core, row)

    flip_half = lambda z, half, core, row: (z, 1 - half, core, row)
    along_z = lambda dz: lambda z, half, core, row: (z + dz, half, core, row)

    weights = conv_in_weight.swapaxes(3, 4).reshape(9, 3, 32, 512)
    zones = [[c, c + 4, c + 8, c + 12] for c in range(4)]

    def to_zones(array):
        pieces = jnp.stack([array[..., 120 * i : 120 * i + 128] for i in range(4)])
        return lax.all_to_all(pieces, "chan", split_axis=0, concat_axis=0, axis_index_groups=zones, tiled=True)

    padded = jnp.pad(latents.transpose(2, 1, 3, 0), ((0, 0), (0, 0), (0, 0), (4, 28)))
    own = to_zones(padded)
    rim = jnp.pad(hidden_rim, ((0, 4), (0, 0), (0, 0), (0, 0))).transpose(1, 2, 0, 3)
    edge_rows = lambda i, j: jnp.concatenate([padded[i].reshape(192, 512), rim[:, j].reshape(128, 512)])
    above, below = send(edge_rows(3, 7), to_row(1)), send(edge_rows(0, 0), to_row(-1))
    odd = row % 2
    near = send(lax.dynamic_slice_in_dim(weights, odd * 256, 256, axis=3), along_z(2))
    own, above, below, weights, near = lax.optimization_barrier((own, above, below, weights, near))

    other = send(own, flip_half)
    w1, w3 = send(weights, along_z(1)), send(weights, along_z(3))
    far = send(near, lambda z, half, core, row: (z, half, core, row ^ 1))
    own_edge = to_zones(jnp.stack([above[:192].reshape(6, 32, 512), below[:192].reshape(6, 32, 512)]))
    other_edge = send(own_edge, flip_half)
    rim_above, rim_below = above[192:].reshape(2, 64, 512), below[192:].reshape(2, 64, 512)
    column = lambda i: jnp.concatenate([rim_above[:, None, i], rim[:, :, i], rim_below[:, None, i]], axis=1)
    before, after = send(column(59), to_chan(1)), send(column(0), to_chan(-1))
    rim = conv_rim(rim, rim_above, rim_below, before, after, conv_out_weight)
    other, other_edge, w1, w3, far, rim = lax.optimization_barrier((other, other_edge, w1, w3, far, rim))
    parts = [own, other, send(own, flip_core), send(other, flip_core),
             own_edge, other_edge, send(own_edge, flip_core), send(other_edge, flip_core)]
    weights = [weights, w1, w3, near, far]

    by_owner = conv_in_bias.reshape(4, 4, 32)
    bias = lax.dynamic_index_in_dim(by_owner, strip, 1, keepdims=False).reshape(128, 1)
    place = jnp.stack([z, half, core, odd]).astype(jnp.int32)
    *strips, stats = conv_in(place, parts, weights, jnp.broadcast_to(bias, (128, 128)))

    parts = strips[:1] + [
        send(strips[r], lambda z, half, core, row: (z, half ^ (r // 2), core ^ (r % 2), row)) for r in range(1, 4)]
    stats, parts[1] = lax.optimization_barrier((stats, parts[1]))
    first = jnp.stack(parts)
    above, below = send(first[:, 3], to_row(1)), send(first[:, 0], to_row(-1))
    gathered = lax.all_to_all(stats, BOTH, split_axis=0, concat_axis=0, tiled=True)
    sums, squares = gathered.reshape(4, 4, 8, 128)[..., :16].sum(axis=(0, 2)).reshape(4, 2, 8).swapaxes(0, 1)
    counted = float(480 * 4 * 32 * 16)
    mean = sums / counted
    var = squares / counted - mean * mean
    inv = 1.0 / jnp.sqrt(var + 1e-06)
    by_place = lambda vector: vector.reshape(4, 4, 32).swapaxes(0, 1).reshape(4, 128)
    vectors = jnp.stack(
        [jnp.repeat(mean, 16, axis=1), jnp.repeat(inv, 16, axis=1) * by_place(norm_gain), by_place(norm_shift)]
        + [jnp.zeros((4, 128), F32)] * 5, axis=1)
    edges = jnp.stack([strip, chan == 0, chan == 15, row == 0, row == 7]).astype(jnp.int32)
    decoded = conv_out(edges, first, above, below, vectors, rim, conv_out_bias.reshape(1, 256),
                       conv_out_weight)
    return decoded.transpose(4, 0, 2, 3, 1, 5)[:30].reshape(60, 4, 8, 256)


def solution(mesh):
    return jax.shard_map(
        body,
        mesh=mesh,
        in_specs=(
            P(None, None, "rows", "chan"),
            P(None, None, None, None, "chan"),
            P(),
            P(),
            P(),
            P("chan", None, "rows", None),
            P(),
            P(),
        ),
        out_specs=P("chan", None, "rows", None),
        check_vma=False,
    )
```

```python
import jax
import jax.numpy as jnp
from jax import lax
from jax.experimental import pallas as pl
from jax.experimental.pallas import tpu as pltpu
from jax.sharding import PartitionSpec as P

GROUPS = 32
BOTH = ("chan", "rows")
BF16 = jnp.bfloat16
F32 = jnp.float32


def device_perm(move):
    pairs = []
    for d in range(128):
        chan, row = divmod(d, 8)
        to = move(chan // 4, chan // 2 % 2, chan % 2, row)
        if to is not None:
            z, half, core, row = to
            pairs.append((d, ((z % 4) * 4 + half * 2 + core) * 8 + row))
    return pairs


def send(array, move):
    return lax.ppermute(array, BOTH, device_perm(move))


def to_row(step):
    return lambda z, half, core, row: (z, half, core, row + step) if 0 <= row + step < 8 else None


def to_chan(step):
    def move(z, half, core, row):
        chan = z * 4 + half * 2 + core + step
        return (chan // 4, chan // 2 % 2, chan % 2, row) if 0 <= chan < 16 else None

    return move


def conv_in_kernel(place, own, other, own_swap, other_swap, own_edge, other_edge, own_edge_swap, other_edge_swap,
                   w0, w1, w3, near, far, bias, strip0, strip1, strip2, strip3, stats,
                   x, w, acc, turned, moments, sems):
    z, half, core, odd = (place[i] for i in range(4))

    def fetch(i, source, target):
        return pltpu.make_async_copy(source, target, sems.at[i])

    groups = []
    for tap, frames in ((0, pl.ds(0, 1)), (1, pl.ds(1, 1)), (2, pl.ds(2, 1)), (None, pl.ds(3, 3))):
        group = []
        for source, ends, dh, owner in (
            (own, own_edge, 0, core), (other, other_edge, 1, core),
            (own_swap, own_edge_swap, 0, 1 - core), (other_swap, other_edge_swap, 1, 1 - core),
        ):
            block = (half + dh) % 2 * 2 + owner
            group.append((source.at[:, :, frames], x.at[:, 1:5, frames, block]))
            for side in range(2):
                group.append((ends.at[:, side, frames], x.at[:, 5 * side, frames, block]))
        if tap is not None:
            taps = pl.ds(3 * tap, 3)
            for dz, source in ((0, w0), (1, w1), (3, w3)):
                group.append((source.at[taps], w.at[taps, :, (z + 4 - dz) % 4]))
            for which, source in ((odd, near), (1 - odd, far)):
                columns = pl.ds(pl.multiple_of(which * 256, 256), 256)
                group.append((source.at[taps], w.at[taps, :, (z + 2) % 4, :, columns]))
        start = sum(len(g) for g in groups)
        groups.append([fetch(start + i, *pair) for i, pair in enumerate(group)])
    for group in groups:
        for copy in group:
            copy.start()
    moments[...] = jnp.zeros_like(moments)
    lane = lax.broadcasted_iota(jnp.int32, (128, 128), 1)
    inside = (lane >= 4) & (lane < 124)

    def frame_tap(t, g, a):
        summed = None
        for b in range(3):
            rhs = jnp.concatenate([x[:, b + g * 2 + h, t + a].reshape(512, 128) for h in range(2)], axis=1)
            lhs = w[a * 3 + b].reshape(384, 512)
            term = jnp.dot(lhs, rhs, preferred_element_type=F32)
            summed = term if summed is None else summed + term
        return summed

    def finish(t, g, summed):
        for h in range(2):
            part = summed[:, h * 128 : (h + 1) * 128]
            value = pltpu.roll(part[0:128], 1, 1) + part[128:256] + pltpu.roll(part[256:384], 127, 1)
            value = (value + bias[...]).astype(BF16).astype(F32)
            kept = jnp.where(inside, value, 0.0)
            moments[0] += kept
            moments[1] += kept * kept
            turned[...] = value.T
            for r, strip in enumerate((strip0, strip1, strip2, strip3)):
                strip[g * 2 + h, t] = turned[pl.ds(3 + 30 * ((half * 2 + core) ^ r), 32), :].astype(BF16)

    def frame(t, _):
        for g in range(2):
            finish(t, g, frame_tap(t, g, 0) + frame_tap(t, g, 1) + frame_tap(t, g, 2))
        return 0

    for a in range(3):
        for copy in groups[a]:
            copy.wait()
        for g in range(2):
            term = frame_tap(0, g, a)
            if a == 0:
                acc[g] = term
            elif a == 1:
                acc[g] += term
            else:
                finish(0, g, acc[g] + term)
    for copy in groups[3]:
        copy.wait()
    lax.fori_loop(1, 4, frame, 0)
    lane, group = (lax.broadcasted_iota(jnp.int32, (8, 128), i) for i in (1, 0))
    row = jnp.zeros((1, 128), F32)
    for i in range(2):
        grouped = jnp.sum(moments[i].reshape(8, 16, 128), axis=1)
        totals = jnp.sum(grouped, axis=1, keepdims=True)
        row += jnp.sum(jnp.where(lane == group + 8 * i, totals, 0.0), axis=0, keepdims=True)
    stats[...] = jnp.broadcast_to(row, (128, 128))


def conv_in(place, parts, weights, bias):
    return pl.pallas_call(
        conv_in_kernel,
        out_shape=[jax.ShapeDtypeStruct((4, 4, 32, 128), BF16)] * 4 + [jax.ShapeDtypeStruct((128, 128), F32)],
        in_specs=[pl.BlockSpec(memory_space=pltpu.SMEM)] + [pl.BlockSpec(memory_space=pl.ANY)] * 13
        + [pl.BlockSpec(memory_space=pltpu.VMEM)],
        out_specs=[pl.BlockSpec(memory_space=pltpu.VMEM)] * 5,
        scratch_shapes=[
            pltpu.VMEM((4, 6, 6, 4, 32, 128), BF16),
            pltpu.VMEM((9, 3, 4, 32, 512), BF16),
            pltpu.VMEM((2, 384, 256), F32),
            pltpu.VMEM((128, 128), F32),
            pltpu.VMEM((2, 128, 128), F32),
            pltpu.SemaphoreType.DMA((63,)),
        ],
        compiler_params=pltpu.CompilerParams(vmem_limit_bytes=56 * 1024 * 1024),
        cost_estimate=pl.CostEstimate(flops=7_200_000_000, bytes_accessed=9_000_000, transcendentals=0),
        name="conv_in",
    )(place, *parts, *weights, bias)


def collapse(taps, out):
    def pairs(t0, t1, t2):
        return ((t0, t1 + t2), (t0 + t1, t2))

    for z in range(4):
        for p in range(4):
            source = z * 128 + p * 32
            target = p * 128 + z * 32
            wide = [[taps[b, c, source : source + 32, :].astype(F32) for c in range(3)] for b in range(3)]
            by_col = [pairs(*row) for row in wide]
            for pw in range(2):
                for side in range(2):
                    by_row = pairs(by_col[0][pw][side], by_col[1][pw][side], by_col[2][pw][side])
                    for ph in range(2):
                        for j in range(2):
                            out[ph, j, pw, side * 512 + target : side * 512 + target + 32, :] = by_row[ph][j].astype(BF16)


def rim_kernel(rim, above, below, before, after, weight, out, w, wide, fine, sem):
    fetch = pltpu.make_async_copy(weight.at[0:2], w, sem)
    fetch.start()
    column = lax.broadcasted_iota(jnp.int32, (64, 512), 0)
    for t in range(2):
        for h in range(10):
            line = above[t] if h == 0 else below[t] if h == 9 else rim[t, h - 1]
            line = pltpu.roll(line.astype(F32), 1, 0)
            line = jnp.where(column == 0, before[t, h : h + 1].astype(F32), line)
            line = jnp.where(column == 61, after[t, h : h + 1].astype(F32), line)
            for s in range(3):
                moved = line if s == 0 else pltpu.roll(line, 64 - s, 0)
                wide[t, h, :, s * 512 : s * 512 + 512] = moved.astype(BF16)
    fetch.wait()
    for t in range(2):
        summed = None
        for a in range(2 - t):
            for b in range(3):
                lhs = wide[t + a, b : b + 8].reshape(512, 1536)
                term = jnp.dot(lhs, w[a, b], preferred_element_type=F32)
                summed = term if summed is None else summed + term
        for c in range(2):
            fine[...] = summed[:, c * 128 : c * 128 + 128].reshape(8, 64, 128)
            for r in range(8):
                for pw in range(2):
                    out[pw, r % 2, t, r // 2, :, c * 128 : c * 128 + 128] = fine[r, pl.ds(pw, 32, stride=2), :]


def conv_rim(rim, above, below, before, after, weight):
    return pl.pallas_call(
        rim_kernel,
        out_shape=jax.ShapeDtypeStruct((2, 2, 2, 4, 32, 256), F32),
        in_specs=[pl.BlockSpec(memory_space=pltpu.VMEM)] * 5 + [pl.BlockSpec(memory_space=pltpu.HBM)],
        out_specs=pl.BlockSpec(memory_space=pltpu.VMEM),
        scratch_shapes=[
            pltpu.VMEM((2, 3, 1536, 256), BF16),
            pltpu.VMEM((2, 10, 64, 1536), BF16),
            pltpu.VMEM((8, 64, 128), F32),
            pltpu.SemaphoreType.DMA,
        ],
        compiler_params=pltpu.CompilerParams(vmem_limit_bytes=50 * 1024 * 1024),
        cost_estimate=pl.CostEstimate(flops=7_200_000_000, bytes_accessed=8_000_000, transcendentals=0),
        name="conv_rim",
    )(rim, above, below, before, after, weight.reshape(3, 3, 1536, 256))


def conv_out_kernel(place, main, up, down, vectors, rim, bias, weight, out, n, acc, raw, w0, w1, w2, sems):
    fetches = [pltpu.make_async_copy(weight.at[tap], raw.at[tap], sems.at[tap]) for tap in range(3)]
    for fetch in fetches:
        fetch.start()
    own, left, right, top, bottom = (place[i] for i in range(5))
    row = lax.broadcasted_iota(jnp.int32, (32, 128), 0)
    keep_col = jnp.where(
        ((row == 0) & (left == 1)) | ((row == 31) & (right == 1)), 0.0, 1.0)
    keep = [keep_col] * 6
    keep[0] = keep_col * jnp.where(top == 1, 0.0, 1.0)
    keep[5] = keep_col * jnp.where(bottom == 1, 0.0, 1.0)

    def frame(t, _):
        for r in range(4):
            p = own ^ r
            vec = vectors[p]
            for h in range(6):
                raw = up[r, t] if h == 0 else down[r, t] if h == 5 else main[r, h - 1, t]
                v = (raw.astype(F32) - vec[0:1]) * vec[1:2] + vec[2:3]
                v = v / (1.0 + jnp.exp(-v)) * keep[h]
                for s in range(3):
                    moved = v if s == 0 else pltpu.roll(v, 32 - s, 0)
                    start = pl.multiple_of(s * 512 + p * 128, 128)
                    n[t, h, :, pl.ds(start, 128)] = moved.astype(BF16)
        return 0

    lax.fori_loop(0, 4, frame, 0)
    whole = jnp.broadcast_to(bias[...], (32, 256))
    for pw in range(2):
        for ph in range(2):
            for t in range(4):
                for h in range(4):
                    acc[pw, ph, t, h] = rim[pw, ph, t, h] + whole if t < 2 else whole

    def multiply(tap, w):
        frames = 2 + tap
        for ph in range(2):
            for j in range(2):
                for pw in range(2):
                    lhs = n[0:frames, ph + j : ph + j + 4, :, pw * 512 : pw * 512 + 1024]
                    term = jnp.dot(lhs.reshape(frames * 128, 1024), w[ph, j, pw], preferred_element_type=F32)
                    acc[pw, ph, 4 - frames : 4] += term.reshape(frames, 4, 32, 256)

    for fetch in fetches:
        fetch.wait()
    collapse(raw.at[2], w2)
    multiply(2, w2)
    collapse(raw.at[1], w1)
    multiply(1, w1)
    collapse(raw.at[0], w0)
    multiply(0, w0)
    out[...] = acc[...].astype(BF16)


def conv_out(place, main, up, down, vectors, rim, bias, weight):
    whole = pl.BlockSpec(memory_space=pltpu.VMEM)
    return pl.pallas_call(
        conv_out_kernel,
        out_shape=jax.ShapeDtypeStruct((2, 2, 4, 4, 32, 256), BF16),
        in_specs=[pl.BlockSpec(memory_space=pltpu.SMEM)] + [whole] * 6 + [pl.BlockSpec(memory_space=pltpu.HBM)],
        out_specs=whole,
        scratch_shapes=[
            pltpu.VMEM((4, 6, 32, 1536), BF16),
            pltpu.VMEM((2, 2, 4, 4, 32, 256), F32),
            pltpu.VMEM((3, 3, 3, 512, 256), BF16),
            pltpu.VMEM((2, 2, 2, 1024, 256), BF16),
            pltpu.VMEM((2, 2, 2, 1024, 256), BF16),
            pltpu.VMEM((2, 2, 2, 1024, 256), BF16),
            pltpu.SemaphoreType.DMA((3,)),
        ],
        compiler_params=pltpu.CompilerParams(vmem_limit_bytes=52 * 1024 * 1024),
        cost_estimate=pl.CostEstimate(flops=4_900_000_000, bytes_accessed=18_000_000, transcendentals=400_000),
        name="conv_out",
    )(place, main, up, down, vectors, rim, bias, weight)


def body(
    latents,
    conv_in_weight,
    conv_in_bias,
    norm_gain,
    norm_shift,
    hidden_rim,
    conv_out_weight,
    conv_out_bias,
):
    chan, row = lax.axis_index("chan"), lax.axis_index("rows")
    z, half, core = chan // 4, chan // 2 % 2, chan % 2
    strip = chan % 4
    flip_core = lambda z, half, core, row: (z, half, 1 - core, row)

    flip_half = lambda z, half, core, row: (z, 1 - half, core, row)
    along_z = lambda dz: lambda z, half, core, row: (z + dz, half, core, row)

    weights = conv_in_weight.swapaxes(3, 4).reshape(9, 3, 32, 512)
    zones = [[c, c + 4, c + 8, c + 12] for c in range(4)]

    def to_zones(array):
        pieces = jnp.stack([array[..., 120 * i : 120 * i + 128] for i in range(4)])
        return lax.all_to_all(pieces, "chan", split_axis=0, concat_axis=0, axis_index_groups=zones, tiled=True)

    padded = jnp.pad(latents.transpose(2, 1, 3, 0), ((0, 0), (0, 0), (0, 0), (4, 28)))
    own = to_zones(padded)
    rim = jnp.pad(hidden_rim, ((0, 4), (0, 0), (0, 0), (0, 0))).transpose(1, 2, 0, 3)
    edge_rows = lambda i, j: jnp.concatenate([padded[i].reshape(192, 512), rim[:, j].reshape(128, 512)])
    above, below = send(edge_rows(3, 7), to_row(1)), send(edge_rows(0, 0), to_row(-1))
    odd = row % 2
    near = send(lax.dynamic_slice_in_dim(weights, odd * 256, 256, axis=3), along_z(2))
    own, weights = lax.optimization_barrier((own, weights))

    other = send(own, flip_half)
    w1, w3 = send(weights, along_z(1)), send(weights, along_z(3))
    far = send(near, lambda z, half, core, row: (z, half, core, row ^ 1))
    own_edge = to_zones(jnp.stack([above[:192].reshape(6, 32, 512), below[:192].reshape(6, 32, 512)]))
    other_edge = send(own_edge, flip_half)
    rim_above, rim_below = above[192:].reshape(2, 64, 512), below[192:].reshape(2, 64, 512)
    column = lambda i: jnp.concatenate([rim_above[:, None, i], rim[:, :, i], rim_below[:, None, i]], axis=1)
    before, after = send(column(59), to_chan(1)), send(column(0), to_chan(-1))
    other, before, after = lax.optimization_barrier((other, before, after))
    rim = conv_rim(rim, rim_above, rim_below, before, after, conv_out_weight)
    other, other_edge, w1, w3, far, rim = lax.optimization_barrier((other, other_edge, w1, w3, far, rim))
    parts = [own, other, send(own, flip_core), send(other, flip_core),
             own_edge, other_edge, send(own_edge, flip_core), send(other_edge, flip_core)]
    weights = [weights, w1, w3, near, far]

    by_owner = conv_in_bias.reshape(4, 4, 32)
    bias = lax.dynamic_index_in_dim(by_owner, strip, 1, keepdims=False).reshape(128, 1)
    place = jnp.stack([z, half, core, odd]).astype(jnp.int32)
    *strips, stats = conv_in(place, parts, weights, jnp.broadcast_to(bias, (128, 128)))

    parts = strips[:1] + [
        send(strips[r], lambda z, half, core, row: (z, half ^ (r // 2), core ^ (r % 2), row)) for r in range(1, 4)]
    stats, parts[1] = lax.optimization_barrier((stats, parts[1]))
    first = jnp.stack(parts)
    above, below = send(first[:, 3], to_row(1)), send(first[:, 0], to_row(-1))
    gathered = lax.all_to_all(stats, BOTH, split_axis=0, concat_axis=0, tiled=True)
    sums, squares = gathered.reshape(4, 4, 8, 128)[..., :16].sum(axis=(0, 2)).reshape(4, 2, 8).swapaxes(0, 1)
    counted = float(480 * 4 * 32 * 16)
    mean = sums / counted
    var = squares / counted - mean * mean
    inv = 1.0 / jnp.sqrt(var + 1e-06)
    by_place = lambda vector: vector.reshape(4, 4, 32).swapaxes(0, 1).reshape(4, 128)
    vectors = jnp.stack(
        [jnp.repeat(mean, 16, axis=1), jnp.repeat(inv, 16, axis=1) * by_place(norm_gain), by_place(norm_shift)]
        + [jnp.zeros((4, 128), F32)] * 5, axis=1)
    edges = jnp.stack([strip, chan == 0, chan == 15, row == 0, row == 7]).astype(jnp.int32)
    decoded = conv_out(edges, first, above, below, vectors, rim, conv_out_bias.reshape(1, 256),
                       conv_out_weight)
    return decoded.transpose(4, 0, 2, 3, 1, 5)[:30].reshape(60, 4, 8, 256)


def solution(mesh):
    return jax.shard_map(
        body,
        mesh=mesh,
        in_specs=(
            P(None, None, "rows", "chan"),
            P(None, None, None, None, "chan"),
            P(),
            P(),
            P(),
            P("chan", None, "rows", None),
            P(),
            P(),
        ),
        out_specs=P("chan", None, "rows", None),
        check_vma=False,
    )
```

```python
import jax
import jax.numpy as jnp
from jax import lax
from jax.experimental import pallas as pl
from jax.experimental.pallas import tpu as pltpu
from jax.sharding import PartitionSpec as P

GROUPS = 32
BOTH = ("chan", "rows")
BF16 = jnp.bfloat16
F32 = jnp.float32


def device_perm(move):
    pairs = []
    for d in range(128):
        chan, row = divmod(d, 8)
        to = move(chan // 4, chan // 2 % 2, chan % 2, row)
        if to is not None:
            z, half, core, row = to
            pairs.append((d, ((z % 4) * 4 + half * 2 + core) * 8 + row))
    return pairs


def send(array, move):
    return lax.ppermute(array, BOTH, device_perm(move))


def to_row(step):
    return lambda z, half, core, row: (z, half, core, row + step) if 0 <= row + step < 8 else None


def to_chan(step):
    def move(z, half, core, row):
        chan = z * 4 + half * 2 + core + step
        return (chan // 4, chan // 2 % 2, chan % 2, row) if 0 <= chan < 16 else None

    return move


def conv_in_kernel(place, own, other, own_swap, other_swap, own_edge, other_edge, own_edge_swap, other_edge_swap,
                   w0, w1, w3, near, far, bias, strip0, strip1, strip2, strip3, stats,
                   x, w, acc, turned, moments, sems):
    z, half, core, odd = (place[i] for i in range(4))

    def fetch(i, source, target):
        return pltpu.make_async_copy(source, target, sems.at[i])

    groups = []
    for tap, frames in ((0, pl.ds(0, 1)), (1, pl.ds(1, 1)), (2, pl.ds(2, 1)), (None, pl.ds(3, 3))):
        group = []
        for source, ends, dh, owner in (
            (own, own_edge, 0, core), (other, other_edge, 1, core),
            (own_swap, own_edge_swap, 0, 1 - core), (other_swap, other_edge_swap, 1, 1 - core),
        ):
            block = (half + dh) % 2 * 2 + owner
            group.append((source.at[:, :, frames], x.at[:, 0:4, frames, block]))
            group.append((ends.at[:, :, frames], x.at[:, 4:6, frames, block]))
        if tap is not None:
            taps = pl.ds(3 * tap, 3)
            for dz, source in ((0, w0), (1, w1), (3, w3)):
                group.append((source.at[taps], w.at[:, tap, :, (z + 4 - dz) % 4]))
            for which, source in ((odd, near), (1 - odd, far)):
                columns = pl.ds(pl.multiple_of(which * 256, 256), 256)
                group.append((source.at[taps], w.at[:, tap, :, (z + 2) % 4, :, columns]))
        start = sum(len(g) for g in groups)
        groups.append([fetch(start + i, *pair) for i, pair in enumerate(group)])
    for group in groups:
        for copy in group:
            copy.start()
    moments[...] = jnp.zeros_like(moments)
    lane = lax.broadcasted_iota(jnp.int32, (128, 128), 1)
    inside = (lane >= 4) & (lane < 124)

    def finish(t, g, summed):
        for h in range(2):
            part = summed[:, h * 128 : (h + 1) * 128]
            value = pltpu.roll(part[0:128], 1, 1) + part[128:256] + pltpu.roll(part[256:384], 127, 1)
            value = (value + bias[...]).astype(BF16).astype(F32)
            kept = jnp.where(inside, value, 0.0)
            moments[0] += kept
            moments[1] += kept * kept
            turned[...] = value.T
            for r, strip in enumerate((strip0, strip1, strip2, strip3)):
                strip[g * 2 + h, t] = turned[pl.ds(3 + 30 * ((half * 2 + core) ^ r), 32), :].astype(BF16)

    for source in range(6):
        if source < 4:
            for copy in groups[source]:
                copy.wait()
        taps = range(max(0, source - 3), min(2, source) + 1)
        for g in range(2):
            summed = None
            for b in range(3):
                rows = [(4, 0, 1, 2, 3, 5)[b + g * 2 + h] for h in range(2)]
                rhs = jnp.concatenate([x[:, r, source].reshape(512, 128) for r in rows], axis=1)
                lhs = w[b, taps[0] : taps[-1] + 1].reshape(len(taps) * 384, 512)
                term = jnp.dot(lhs, rhs, preferred_element_type=F32)
                summed = term if summed is None else summed + term
            for i, a in enumerate(taps):
                t = source - a
                part = summed[i * 384 : i * 384 + 384]
                if a == 0:
                    acc[t, g] = part
                elif a == 1:
                    acc[t, g] += part
                else:
                    finish(t, g, acc[t, g] + part)
    lane, group = (lax.broadcasted_iota(jnp.int32, (8, 128), i) for i in (1, 0))
    row = jnp.zeros((1, 128), F32)
    for i in range(2):
        grouped = jnp.sum(moments[i].reshape(8, 16, 128), axis=1)
        totals = jnp.sum(grouped, axis=1, keepdims=True)
        row += jnp.sum(jnp.where(lane == group + 8 * i, totals, 0.0), axis=0, keepdims=True)
    stats[...] = jnp.broadcast_to(row, (128, 128))


def conv_in(place, parts, weights, bias):
    return pl.pallas_call(
        conv_in_kernel,
        out_shape=[jax.ShapeDtypeStruct((4, 4, 32, 128), BF16)] * 4 + [jax.ShapeDtypeStruct((128, 128), F32)],
        in_specs=[pl.BlockSpec(memory_space=pltpu.SMEM)] + [pl.BlockSpec(memory_space=pl.ANY)] * 13
        + [pl.BlockSpec(memory_space=pltpu.VMEM)],
        out_specs=[pl.BlockSpec(memory_space=pltpu.VMEM)] * 5,
        scratch_shapes=[
            pltpu.VMEM((4, 6, 6, 4, 32, 128), BF16),
            pltpu.VMEM((3, 3, 3, 4, 32, 512), BF16),
            pltpu.VMEM((4, 2, 384, 256), F32),
            pltpu.VMEM((128, 128), F32),
            pltpu.VMEM((2, 128, 128), F32),
            pltpu.SemaphoreType.DMA((47,)),
        ],
        compiler_params=pltpu.CompilerParams(vmem_limit_bytes=56 * 1024 * 1024),
        cost_estimate=pl.CostEstimate(flops=7_200_000_000, bytes_accessed=9_000_000, transcendentals=0),
        name="conv_in",
    )(place, *parts, *weights, bias)


def collapse(taps, out):
    def pairs(t0, t1, t2):
        return ((t0, t1 + t2), (t0 + t1, t2))

    for z in range(4):
        for p in range(4):
            source = z * 128 + p * 32
            target = p * 128 + z * 32
            wide = [[taps[b, c, source : source + 32, :].astype(F32) for c in range(3)] for b in range(3)]
            by_col = [pairs(*row) for row in wide]
            for pw in range(2):
                for side in range(2):
                    by_row = pairs(by_col[0][pw][side], by_col[1][pw][side], by_col[2][pw][side])
                    for ph in range(2):
                        for j in range(2):
                            out[ph, j, pw, side * 512 + target : side * 512 + target + 32, :] = by_row[ph][j].astype(BF16)


def rim_kernel(rim, above, below, before, after, weight, out, w, wide, fine, sem):
    fetch = pltpu.make_async_copy(weight.at[0:2], w, sem)
    fetch.start()
    column = lax.broadcasted_iota(jnp.int32, (64, 512), 0)
    for t in range(2):
        for h in range(10):
            line = above[t] if h == 0 else below[t] if h == 9 else rim[t, h - 1]
            line = pltpu.roll(line.astype(F32), 1, 0)
            line = jnp.where(column == 0, before[t, h : h + 1].astype(F32), line)
            line = jnp.where(column == 61, after[t, h : h + 1].astype(F32), line)
            for s in range(3):
                moved = line if s == 0 else pltpu.roll(line, 64 - s, 0)
                wide[t, h, :, s * 512 : s * 512 + 512] = moved.astype(BF16)
    fetch.wait()
    for t in range(2):
        summed = None
        for a in range(2 - t):
            for b in range(3):
                lhs = wide[t + a, b : b + 8].reshape(512, 1536)
                term = jnp.dot(lhs, w[a, b], preferred_element_type=F32)
                summed = term if summed is None else summed + term
        for c in range(2):
            fine[...] = summed[:, c * 128 : c * 128 + 128].reshape(8, 64, 128)
            for r in range(8):
                for pw in range(2):
                    out[pw, r % 2, t, r // 2, :, c * 128 : c * 128 + 128] = fine[r, pl.ds(pw, 32, stride=2), :]


def conv_rim(rim, above, below, before, after, weight):
    return pl.pallas_call(
        rim_kernel,
        out_shape=jax.ShapeDtypeStruct((2, 2, 2, 4, 32, 256), F32),
        in_specs=[pl.BlockSpec(memory_space=pltpu.VMEM)] * 5 + [pl.BlockSpec(memory_space=pltpu.HBM)],
        out_specs=pl.BlockSpec(memory_space=pltpu.VMEM),
        scratch_shapes=[
            pltpu.VMEM((2, 3, 1536, 256), BF16),
            pltpu.VMEM((2, 10, 64, 1536), BF16),
            pltpu.VMEM((8, 64, 128), F32),
            pltpu.SemaphoreType.DMA,
        ],
        compiler_params=pltpu.CompilerParams(vmem_limit_bytes=50 * 1024 * 1024),
        cost_estimate=pl.CostEstimate(flops=7_200_000_000, bytes_accessed=8_000_000, transcendentals=0),
        name="conv_rim",
    )(rim, above, below, before, after, weight.reshape(3, 3, 1536, 256))


def conv_out_kernel(place, main, up, down, vectors, rim, bias, weight, out, n, acc, raw, w0, w1, w2, sems):
    fetches = [pltpu.make_async_copy(weight.at[tap], raw.at[tap], sems.at[tap]) for tap in range(3)]
    for fetch in fetches:
        fetch.start()
    own, left, right, top, bottom = (place[i] for i in range(5))
    row = lax.broadcasted_iota(jnp.int32, (32, 128), 0)
    keep_col = jnp.where(
        ((row == 0) & (left == 1)) | ((row == 31) & (right == 1)), 0.0, 1.0)
    keep = [keep_col] * 6
    keep[0] = keep_col * jnp.where(top == 1, 0.0, 1.0)
    keep[5] = keep_col * jnp.where(bottom == 1, 0.0, 1.0)

    def frame(t, _):
        for r in range(4):
            p = own ^ r
            vec = vectors[p]
            for h in range(6):
                raw = up[r, t] if h == 0 else down[r, t] if h == 5 else main[r, h - 1, t]
                v = (raw.astype(F32) - vec[0:1]) * vec[1:2] + vec[2:3]
                v = v / (1.0 + jnp.exp(-v)) * keep[h]
                for s in range(3):
                    moved = v if s == 0 else pltpu.roll(v, 32 - s, 0)
                    start = pl.multiple_of(s * 512 + p * 128, 128)
                    n[t, h, :, pl.ds(start, 128)] = moved.astype(BF16)
        return 0

    lax.fori_loop(0, 4, frame, 0)
    whole = jnp.broadcast_to(bias[...], (32, 256))
    for pw in range(2):
        for ph in range(2):
            for t in range(4):
                for h in range(4):
                    acc[pw, ph, t, h] = rim[pw, ph, t, h] + whole if t < 2 else whole

    def multiply(tap, w):
        frames = 2 + tap
        for ph in range(2):
            for j in range(2):
                for pw in range(2):
                    lhs = n[0:frames, ph + j : ph + j + 4, :, pw * 512 : pw * 512 + 1024]
                    term = jnp.dot(lhs.reshape(frames * 128, 1024), w[ph, j, pw], preferred_element_type=F32)
                    acc[pw, ph, 4 - frames : 4] += term.reshape(frames, 4, 32, 256)

    for fetch in fetches:
        fetch.wait()
    collapse(raw.at[2], w2)
    multiply(2, w2)
    collapse(raw.at[1], w1)
    multiply(1, w1)
    collapse(raw.at[0], w0)
    multiply(0, w0)
    for pw in range(2):
        for t in range(4):
            rows = jnp.concatenate([acc[pw, r % 2, t, r // 2][None] for r in range(8)])
            out[:, pw, t] = jnp.swapaxes(rows, 0, 1)[:30].astype(BF16)


def conv_out(place, main, up, down, vectors, rim, bias, weight):
    whole = pl.BlockSpec(memory_space=pltpu.VMEM)
    return pl.pallas_call(
        conv_out_kernel,
        out_shape=jax.ShapeDtypeStruct((30, 2, 4, 8, 256), BF16),
        in_specs=[pl.BlockSpec(memory_space=pltpu.SMEM)] + [whole] * 6 + [pl.BlockSpec(memory_space=pltpu.HBM)],
        out_specs=whole,
        scratch_shapes=[
            pltpu.VMEM((4, 6, 32, 1536), BF16),
            pltpu.VMEM((2, 2, 4, 4, 32, 256), F32),
            pltpu.VMEM((3, 3, 3, 512, 256), BF16),
            pltpu.VMEM((2, 2, 2, 1024, 256), BF16),
            pltpu.VMEM((2, 2, 2, 1024, 256), BF16),
            pltpu.VMEM((2, 2, 2, 1024, 256), BF16),
            pltpu.SemaphoreType.DMA((3,)),
        ],
        compiler_params=pltpu.CompilerParams(vmem_limit_bytes=52 * 1024 * 1024),
        cost_estimate=pl.CostEstimate(flops=4_900_000_000, bytes_accessed=18_000_000, transcendentals=400_000),
        name="conv_out",
    )(place, main, up, down, vectors, rim, bias, weight)


def body(
    latents,
    conv_in_weight,
    conv_in_bias,
    norm_gain,
    norm_shift,
    hidden_rim,
    conv_out_weight,
    conv_out_bias,
):
    chan, row = lax.axis_index("chan"), lax.axis_index("rows")
    z, half, core = chan // 4, chan // 2 % 2, chan % 2
    strip = chan % 4
    flip_core = lambda z, half, core, row: (z, half, 1 - core, row)

    flip_half = lambda z, half, core, row: (z, 1 - half, core, row)
    along_z = lambda dz: lambda z, half, core, row: (z + dz, half, core, row)

    weights = conv_in_weight.swapaxes(3, 4).reshape(9, 3, 32, 512)
    zones = [[c, c + 4, c + 8, c + 12] for c in range(4)]

    def to_zones(array):
        pieces = jnp.stack([array[..., 120 * i : 120 * i + 128] for i in range(4)])
        return lax.all_to_all(pieces, "chan", split_axis=0, concat_axis=0, axis_index_groups=zones, tiled=True)

    padded = jnp.pad(latents.transpose(2, 1, 3, 0), ((0, 0), (0, 0), (0, 0), (4, 28)))
    own = to_zones(padded)
    rim = jnp.pad(hidden_rim, ((0, 4), (0, 0), (0, 0), (0, 0))).transpose(1, 2, 0, 3)
    edge_rows = lambda i, j: jnp.concatenate([padded[i].reshape(192, 512), rim[:, j].reshape(128, 512)])
    above, below = send(edge_rows(3, 7), to_row(1)), send(edge_rows(0, 0), to_row(-1))
    odd = row % 2
    near = send(lax.dynamic_slice_in_dim(weights, odd * 256, 256, axis=3), along_z(2))
    own, weights = lax.optimization_barrier((own, weights))

    other = send(own, flip_half)
    w1, w3 = send(weights, along_z(1)), send(weights, along_z(3))
    far = send(near, lambda z, half, core, row: (z, half, core, row ^ 1))
    own_edge = to_zones(jnp.stack([above[:192].reshape(6, 32, 512), below[:192].reshape(6, 32, 512)]))
    other_edge = send(own_edge, flip_half)
    rim_above, rim_below = above[192:].reshape(2, 64, 512), below[192:].reshape(2, 64, 512)
    column = lambda i: jnp.concatenate([rim_above[:, None, i], rim[:, :, i], rim_below[:, None, i]], axis=1)
    before, after = send(column(59), to_chan(1)), send(column(0), to_chan(-1))
    other, before, after = lax.optimization_barrier((other, before, after))
    rim = conv_rim(rim, rim_above, rim_below, before, after, conv_out_weight)
    other, other_edge, w1, w3, far, rim = lax.optimization_barrier((other, other_edge, w1, w3, far, rim))
    parts = [own, other, send(own, flip_core), send(other, flip_core),
             own_edge, other_edge, send(own_edge, flip_core), send(other_edge, flip_core)]
    weights = [weights, w1, w3, near, far]

    by_owner = conv_in_bias.reshape(4, 4, 32)
    bias = lax.dynamic_index_in_dim(by_owner, strip, 1, keepdims=False).reshape(128, 1)
    place = jnp.stack([z, half, core, odd]).astype(jnp.int32)
    *strips, stats = conv_in(place, parts, weights, jnp.broadcast_to(bias, (128, 128)))

    parts = strips[:1] + [
        send(strips[r], lambda z, half, core, row: (z, half ^ (r // 2), core ^ (r % 2), row)) for r in range(1, 4)]
    stats, parts[1] = lax.optimization_barrier((stats, parts[1]))
    first = jnp.stack(parts)
    above, below = send(first[:, 3], to_row(1)), send(first[:, 0], to_row(-1))
    gathered = lax.all_to_all(stats, BOTH, split_axis=0, concat_axis=0, tiled=True)
    sums, squares = gathered.reshape(4, 4, 8, 128)[..., :16].sum(axis=(0, 2)).reshape(4, 2, 8).swapaxes(0, 1)
    counted = float(480 * 4 * 32 * 16)
    mean = sums / counted
    var = squares / counted - mean * mean
    inv = 1.0 / jnp.sqrt(var + 1e-06)
    by_place = lambda vector: vector.reshape(4, 4, 32).swapaxes(0, 1).reshape(4, 128)
    vectors = jnp.stack(
        [jnp.repeat(mean, 16, axis=1), jnp.repeat(inv, 16, axis=1) * by_place(norm_gain), by_place(norm_shift)]
        + [jnp.zeros((4, 128), F32)] * 5, axis=1)
    edges = jnp.stack([strip, chan == 0, chan == 15, row == 0, row == 7]).astype(jnp.int32)
    decoded = conv_out(edges, first, above, below, vectors, rim, conv_out_bias.reshape(1, 256),
                       conv_out_weight)
    return decoded.reshape(60, 4, 8, 256)


def solution(mesh):
    return jax.shard_map(
        body,
        mesh=mesh,
        in_specs=(
            P(None, None, "rows", "chan"),
            P(None, None, None, None, "chan"),
            P(),
            P(),
            P(),
            P("chan", None, "rows", None),
            P(),
            P(),
        ),
        out_specs=P("chan", None, "rows", None),
        check_vma=False,
    )
```

```python
import jax
import jax.numpy as jnp
from jax import lax
from jax.experimental import pallas as pl
from jax.experimental.pallas import tpu as pltpu
from jax.sharding import PartitionSpec as P

GROUPS = 32
BOTH = ("chan", "rows")
BF16 = jnp.bfloat16
F32 = jnp.float32


def device_perm(move):
    pairs = []
    for d in range(128):
        chan, row = divmod(d, 8)
        to = move(chan // 4, chan // 2 % 2, chan % 2, row)
        if to is not None:
            z, half, core, row = to
            pairs.append((d, ((z % 4) * 4 + half * 2 + core) * 8 + row))
    return pairs


def send(array, move):
    return lax.ppermute(array, BOTH, device_perm(move))


def to_row(step):
    return lambda z, half, core, row: (z, half, core, row + step) if 0 <= row + step < 8 else None


def to_chan(step):
    def move(z, half, core, row):
        chan = z * 4 + half * 2 + core + step
        return (chan // 4, chan // 2 % 2, chan % 2, row) if 0 <= chan < 16 else None

    return move


def conv_in_kernel(place, own, other, own_swap, other_swap, own_edge, other_edge, own_edge_swap, other_edge_swap,
                   w0, w1, w3, near, far, bias, strip0, strip1, strip2, strip3, stats,
                   x, w, acc, turned, moments, sems):
    z, half, core, odd = (place[i] for i in range(4))

    def fetch(i, source, target):
        return pltpu.make_async_copy(source, target, sems.at[i])

    groups = []
    for tap, frames in ((0, pl.ds(0, 1)), (1, pl.ds(1, 1)), (2, pl.ds(2, 1)), (None, pl.ds(3, 3))):
        group = []
        for source, ends, dh, owner in (
            (own, own_edge, 0, core), (other, other_edge, 1, core),
            (own_swap, own_edge_swap, 0, 1 - core), (other_swap, other_edge_swap, 1, 1 - core),
        ):
            block = (half + dh) % 2 * 2 + owner
            group.append((source.at[:, :, frames], x.at[:, 0:4, frames, block]))
            group.append((ends.at[:, :, frames], x.at[:, 4:6, frames, block]))
        if tap is not None:
            taps = pl.ds(3 * tap, 3)
            for dz, source in ((0, w0), (1, w1), (3, w3)):
                group.append((source.at[taps], w.at[:, tap, :, (z + 4 - dz) % 4]))
            for which, source in ((odd, near), (1 - odd, far)):
                columns = pl.ds(pl.multiple_of(which * 256, 256), 256)
                group.append((source.at[taps], w.at[:, tap, :, (z + 2) % 4, :, columns]))
        start = sum(len(g) for g in groups)
        groups.append([fetch(start + i, *pair) for i, pair in enumerate(group)])
    for group in groups:
        for copy in group:
            copy.start()
    moments[...] = jnp.zeros_like(moments)
    lane = lax.broadcasted_iota(jnp.int32, (128, 128), 1)
    inside = (lane >= 4) & (lane < 124)

    def finish(t, g, summed):
        for h in range(2):
            part = summed[:, h * 128 : (h + 1) * 128]
            value = pltpu.roll(part[0:128], 1, 1) + part[128:256] + pltpu.roll(part[256:384], 127, 1)
            value = (value + bias[...]).astype(BF16).astype(F32)
            kept = jnp.where(inside, value, 0.0)
            moments[0] += kept
            moments[1] += kept * kept
            turned[...] = value.T
            for r, strip in enumerate((strip0, strip1, strip2, strip3)):
                strip[g * 2 + h, t] = turned[pl.ds(3 + 30 * ((half * 2 + core) ^ r), 32), :].astype(BF16)

    for source in range(6):
        if source < 4:
            for copy in groups[source]:
                copy.wait()
        taps = range(max(0, source - 3), min(2, source) + 1)
        for g in range(2):
            summed = None
            for b in range(3):
                rows = [(4, 0, 1, 2, 3, 5)[b + g * 2 + h] for h in range(2)]
                rhs = jnp.concatenate([x[:, r, source].reshape(512, 128) for r in rows], axis=1)
                lhs = w[b, taps[0] : taps[-1] + 1].reshape(len(taps) * 384, 512)
                term = jnp.dot(lhs, rhs, preferred_element_type=F32)
                summed = term if summed is None else summed + term
            for i, a in enumerate(taps):
                t = source - a
                part = summed[i * 384 : i * 384 + 384]
                if a == 0:
                    acc[t, g] = part
                elif a == 1:
                    acc[t, g] += part
                else:
                    finish(t, g, acc[t, g] + part)
    lane, group = (lax.broadcasted_iota(jnp.int32, (8, 128), i) for i in (1, 0))
    row = jnp.zeros((1, 128), F32)
    for i in range(2):
        grouped = jnp.sum(moments[i].reshape(8, 16, 128), axis=1)
        totals = jnp.sum(grouped, axis=1, keepdims=True)
        row += jnp.sum(jnp.where(lane == group + 8 * i, totals, 0.0), axis=0, keepdims=True)
    stats[...] = jnp.broadcast_to(row, (128, 128))


def conv_in(place, parts, weights, bias):
    return pl.pallas_call(
        conv_in_kernel,
        out_shape=[jax.ShapeDtypeStruct((4, 4, 32, 128), BF16)] * 4 + [jax.ShapeDtypeStruct((128, 128), F32)],
        in_specs=[pl.BlockSpec(memory_space=pltpu.SMEM)] + [pl.BlockSpec(memory_space=pl.ANY)] * 13
        + [pl.BlockSpec(memory_space=pltpu.VMEM)],
        out_specs=[pl.BlockSpec(memory_space=pltpu.VMEM)] * 5,
        scratch_shapes=[
            pltpu.VMEM((4, 6, 6, 4, 32, 128), BF16),
            pltpu.VMEM((3, 3, 3, 4, 32, 512), BF16),
            pltpu.VMEM((4, 2, 384, 256), F32),
            pltpu.VMEM((128, 128), F32),
            pltpu.VMEM((2, 128, 128), F32),
            pltpu.SemaphoreType.DMA((47,)),
        ],
        compiler_params=pltpu.CompilerParams(vmem_limit_bytes=56 * 1024 * 1024),
        cost_estimate=pl.CostEstimate(flops=7_200_000_000, bytes_accessed=9_000_000, transcendentals=0),
        name="conv_in",
    )(place, *parts, *weights, bias)


def collapse(taps, out):
    def pairs(t0, t1, t2):
        return ((t0, t1 + t2), (t0 + t1, t2))

    for z in range(4):
        for p in range(4):
            source = z * 128 + p * 32
            target = p * 128 + z * 32
            wide = [[taps[b, c, source : source + 32, :].astype(F32) for c in range(3)] for b in range(3)]
            by_col = [pairs(*row) for row in wide]
            for pw in range(2):
                for side in range(2):
                    by_row = pairs(by_col[0][pw][side], by_col[1][pw][side], by_col[2][pw][side])
                    for ph in range(2):
                        for j in range(2):
                            out[ph, j, pw, side * 512 + target : side * 512 + target + 32, :] = by_row[ph][j].astype(BF16)


def rim_kernel(rim, above, below, before, after, weight, out, w, wide, fine, sem):
    fetch = pltpu.make_async_copy(weight.at[0:2], w, sem)
    fetch.start()
    column = lax.broadcasted_iota(jnp.int32, (64, 512), 0)
    for t in range(2):
        for h in range(10):
            line = above[t] if h == 0 else below[t] if h == 9 else rim[t, h - 1]
            line = pltpu.roll(line.astype(F32), 1, 0)
            line = jnp.where(column == 0, before[t, h : h + 1].astype(F32), line)
            line = jnp.where(column == 61, after[t, h : h + 1].astype(F32), line)
            for s in range(3):
                moved = line if s == 0 else pltpu.roll(line, 64 - s, 0)
                wide[t, h, :, s * 512 : s * 512 + 512] = moved.astype(BF16)
    fetch.wait()
    for t in range(2):
        summed = None
        for a in range(2 - t):
            for b in range(3):
                lhs = wide[t + a, b : b + 8].reshape(512, 1536)
                term = jnp.dot(lhs, w[a, b], preferred_element_type=F32)
                summed = term if summed is None else summed + term
        for c in range(2):
            fine[...] = summed[:, c * 128 : c * 128 + 128].reshape(8, 64, 128)
            for r in range(8):
                for pw in range(2):
                    out[pw, r % 2, t, r // 2, :, c * 128 : c * 128 + 128] = fine[r, pl.ds(pw, 32, stride=2), :]


def conv_rim(rim, above, below, before, after, weight):
    return pl.pallas_call(
        rim_kernel,
        out_shape=jax.ShapeDtypeStruct((2, 2, 2, 4, 32, 256), F32),
        in_specs=[pl.BlockSpec(memory_space=pltpu.VMEM)] * 5 + [pl.BlockSpec(memory_space=pltpu.HBM)],
        out_specs=pl.BlockSpec(memory_space=pltpu.VMEM),
        scratch_shapes=[
            pltpu.VMEM((2, 3, 1536, 256), BF16),
            pltpu.VMEM((2, 10, 64, 1536), BF16),
            pltpu.VMEM((8, 64, 128), F32),
            pltpu.SemaphoreType.DMA,
        ],
        compiler_params=pltpu.CompilerParams(vmem_limit_bytes=50 * 1024 * 1024),
        cost_estimate=pl.CostEstimate(flops=7_200_000_000, bytes_accessed=8_000_000, transcendentals=0),
        name="conv_rim",
    )(rim, above, below, before, after, weight.reshape(3, 3, 1536, 256))


def conv_out_kernel(place, main, up, down, vectors, rim, bias, weight, out, n, acc, raw, w0, w1, w2, sems):
    fetches = [pltpu.make_async_copy(weight.at[tap], raw.at[tap], sems.at[tap]) for tap in range(3)]
    for fetch in fetches:
        fetch.start()
    own, left, right, top, bottom = (place[i] for i in range(5))
    row = lax.broadcasted_iota(jnp.int32, (32, 128), 0)
    keep_col = jnp.where(
        ((row == 0) & (left == 1)) | ((row == 31) & (right == 1)), 0.0, 1.0)
    keep = [keep_col] * 6
    keep[0] = keep_col * jnp.where(top == 1, 0.0, 1.0)
    keep[5] = keep_col * jnp.where(bottom == 1, 0.0, 1.0)

    def frame(t, _):
        for r in range(4):
            p = own ^ r
            vec = vectors[p]
            for h in range(6):
                raw = up[r, t] if h == 0 else down[r, t] if h == 5 else main[r, h - 1, t]
                v = (raw.astype(F32) - vec[0:1]) * vec[1:2] + vec[2:3]
                v = v / (1.0 + jnp.exp(-v)) * keep[h]
                for s in range(3):
                    moved = v if s == 0 else pltpu.roll(v, 32 - s, 0)
                    start = pl.multiple_of(s * 512 + p * 128, 128)
                    n[t, h, :, pl.ds(start, 128)] = moved.astype(BF16)
        return 0

    lax.fori_loop(0, 4, frame, 0)
    whole = jnp.broadcast_to(bias[...], (32, 256))
    for pw in range(2):
        for ph in range(2):
            for t in range(4):
                for h in range(4):
                    acc[pw, ph, t, h] = rim[pw, ph, t, h] + whole if t < 2 else whole

    def multiply(tap, w):
        frames = 2 + tap
        for ph in range(2):
            for j in range(2):
                for pw in range(2):
                    lhs = n[0:frames, ph + j : ph + j + 4, :, pw * 512 : pw * 512 + 1024]
                    term = jnp.dot(lhs.reshape(frames * 128, 1024), w[ph, j, pw], preferred_element_type=F32)
                    acc[pw, ph, 4 - frames : 4] += term.reshape(frames, 4, 32, 256)

    for fetch in fetches:
        fetch.wait()
    collapse(raw.at[2], w2)
    multiply(2, w2)
    collapse(raw.at[1], w1)
    multiply(1, w1)
    collapse(raw.at[0], w0)
    multiply(0, w0)
    for pw in range(2):
        for t in range(4):
            rows = jnp.concatenate([acc[pw, r % 2, t, r // 2][None] for r in range(8)])
            out[:, pw, t] = jnp.swapaxes(rows, 0, 1)[:30].astype(BF16)


def conv_out(place, main, up, down, vectors, rim, bias, weight):
    whole = pl.BlockSpec(memory_space=pltpu.VMEM)
    return pl.pallas_call(
        conv_out_kernel,
        out_shape=jax.ShapeDtypeStruct((30, 2, 4, 8, 256), BF16),
        in_specs=[pl.BlockSpec(memory_space=pltpu.SMEM)] + [whole] * 6 + [pl.BlockSpec(memory_space=pltpu.HBM)],
        out_specs=whole,
        scratch_shapes=[
            pltpu.VMEM((4, 6, 32, 1536), BF16),
            pltpu.VMEM((2, 2, 4, 4, 32, 256), F32),
            pltpu.VMEM((3, 3, 3, 512, 256), BF16),
            pltpu.VMEM((2, 2, 2, 1024, 256), BF16),
            pltpu.VMEM((2, 2, 2, 1024, 256), BF16),
            pltpu.VMEM((2, 2, 2, 1024, 256), BF16),
            pltpu.SemaphoreType.DMA((3,)),
        ],
        compiler_params=pltpu.CompilerParams(vmem_limit_bytes=52 * 1024 * 1024),
        cost_estimate=pl.CostEstimate(flops=4_900_000_000, bytes_accessed=18_000_000, transcendentals=400_000),
        name="conv_out",
    )(place, main, up, down, vectors, rim, bias, weight)


def body(
    latents,
    conv_in_weight,
    conv_in_bias,
    norm_gain,
    norm_shift,
    hidden_rim,
    conv_out_weight,
    conv_out_bias,
):
    chan, row = lax.axis_index("chan"), lax.axis_index("rows")
    z, half, core = chan // 4, chan // 2 % 2, chan % 2
    strip = chan % 4
    flip_core = lambda z, half, core, row: (z, half, 1 - core, row)

    flip_half = lambda z, half, core, row: (z, 1 - half, core, row)
    along_z = lambda dz: lambda z, half, core, row: (z + dz, half, core, row)

    weights = conv_in_weight.swapaxes(3, 4).reshape(9, 3, 32, 512)
    zones = [[c, c + 4, c + 8, c + 12] for c in range(4)]

    def to_zones(array):
        pieces = jnp.stack([array[..., 120 * i : 120 * i + 128] for i in range(4)])
        return lax.all_to_all(pieces, "chan", split_axis=0, concat_axis=0, axis_index_groups=zones, tiled=True)

    padded = jnp.pad(latents.transpose(2, 1, 3, 0), ((0, 0), (0, 0), (0, 0), (4, 28)))
    own = to_zones(padded)
    rim = jnp.pad(hidden_rim, ((0, 4), (0, 0), (0, 0), (0, 0))).transpose(1, 2, 0, 3)
    edge_rows = lambda i, j: jnp.concatenate([padded[i].reshape(192, 512), rim[:, j].reshape(128, 512)])
    above, below = send(edge_rows(3, 7), to_row(1)), send(edge_rows(0, 0), to_row(-1))
    odd = row % 2
    near = send(lax.dynamic_slice_in_dim(weights, odd * 256, 256, axis=3), along_z(2))
    own, weights = lax.optimization_barrier((own, weights))

    other = send(own, flip_half)
    w1, w3 = send(weights, along_z(1)), send(weights, along_z(3))
    far = send(near, lambda z, half, core, row: (z, half, core, row ^ 1))
    own_edge = to_zones(jnp.stack([above[:192].reshape(6, 32, 512), below[:192].reshape(6, 32, 512)]))
    other_edge = send(own_edge, flip_half)
    rim_above, rim_below = above[192:].reshape(2, 64, 512), below[192:].reshape(2, 64, 512)
    column = lambda i: jnp.concatenate([rim_above[:, None, i], rim[:, :, i], rim_below[:, None, i]], axis=1)
    before, after = send(column(59), to_chan(1)), send(column(0), to_chan(-1))
    other, before, after = lax.optimization_barrier((other, before, after))
    rim = conv_rim(rim, rim_above, rim_below, before, after, conv_out_weight)
    rim, own_late = lax.optimization_barrier((rim, own))
    own_swap = send(own_late, flip_core)
    other, other_edge, w1, w3, far, rim = lax.optimization_barrier((other, other_edge, w1, w3, far, rim))
    parts = [own, other, own_swap, send(other, flip_core),
             own_edge, other_edge, send(own_edge, flip_core), send(other_edge, flip_core)]
    weights = [weights, w1, w3, near, far]

    by_owner = conv_in_bias.reshape(4, 4, 32)
    bias = lax.dynamic_index_in_dim(by_owner, strip, 1, keepdims=False).reshape(128, 1)
    place = jnp.stack([z, half, core, odd]).astype(jnp.int32)
    *strips, stats = conv_in(place, parts, weights, jnp.broadcast_to(bias, (128, 128)))

    parts = strips[:1] + [
        send(strips[r], lambda z, half, core, row: (z, half ^ (r // 2), core ^ (r % 2), row)) for r in range(1, 4)]
    stats, parts[1] = lax.optimization_barrier((stats, parts[1]))
    first = jnp.stack(parts)
    above, below = send(first[:, 3], to_row(1)), send(first[:, 0], to_row(-1))
    gathered = lax.all_to_all(stats, BOTH, split_axis=0, concat_axis=0, tiled=True)
    sums, squares = gathered.reshape(4, 4, 8, 128)[..., :16].sum(axis=(0, 2)).reshape(4, 2, 8).swapaxes(0, 1)
    counted = float(480 * 4 * 32 * 16)
    mean = sums / counted
    var = squares / counted - mean * mean
    inv = 1.0 / jnp.sqrt(var + 1e-06)
    by_place = lambda vector: vector.reshape(4, 4, 32).swapaxes(0, 1).reshape(4, 128)
    vectors = jnp.stack(
        [jnp.repeat(mean, 16, axis=1), jnp.repeat(inv, 16, axis=1) * by_place(norm_gain), by_place(norm_shift)]
        + [jnp.zeros((4, 128), F32)] * 5, axis=1)
    edges = jnp.stack([strip, chan == 0, chan == 15, row == 0, row == 7]).astype(jnp.int32)
    decoded = conv_out(edges, first, above, below, vectors, rim, conv_out_bias.reshape(1, 256),
                       conv_out_weight)
    return decoded.reshape(60, 4, 8, 256)


def solution(mesh):
    return jax.shard_map(
        body,
        mesh=mesh,
        in_specs=(
            P(None, None, "rows", "chan"),
            P(None, None, None, None, "chan"),
            P(),
            P(),
            P(),
            P("chan", None, "rows", None),
            P(),
            P(),
        ),
        out_specs=P("chan", None, "rows", None),
        check_vma=False,
    )
```

```python
import jax
import jax.numpy as jnp
from jax import lax
from jax.experimental import pallas as pl
from jax.experimental.pallas import tpu as pltpu
from jax.sharding import PartitionSpec as P

GROUPS = 32
BOTH = ("chan", "rows")
BF16 = jnp.bfloat16
F32 = jnp.float32


def device_perm(move):
    pairs = []
    for d in range(128):
        chan, row = divmod(d, 8)
        to = move(chan // 4, chan // 2 % 2, chan % 2, row)
        if to is not None:
            z, half, core, row = to
            pairs.append((d, ((z % 4) * 4 + half * 2 + core) * 8 + row))
    return pairs


def send(array, move):
    return lax.ppermute(array, BOTH, device_perm(move))


def to_row(step):
    return lambda z, half, core, row: (z, half, core, row + step) if 0 <= row + step < 8 else None


def to_chan(step):
    def move(z, half, core, row):
        chan = z * 4 + half * 2 + core + step
        return (chan // 4, chan // 2 % 2, chan % 2, row) if 0 <= chan < 16 else None

    return move


def conv_in_kernel(place, own, other, own_swap, other_swap, own_edge, other_edge, own_edge_swap, other_edge_swap,
                   w0, w1, w3, near, far, bias, strip0, strip1, strip2, strip3, stats,
                   x, w, acc, turned, moments, sems):
    z, half, core, odd = (place[i] for i in range(4))

    def fetch(i, source, target):
        return pltpu.make_async_copy(source, target, sems.at[i])

    groups = []
    for tap, frames in ((0, pl.ds(0, 1)), (1, pl.ds(1, 1)), (2, pl.ds(2, 1)), (None, pl.ds(3, 3))):
        group = []
        for source, ends, dh, owner in (
            (own, own_edge, 0, core), (other, other_edge, 1, core),
            (own_swap, own_edge_swap, 0, 1 - core), (other_swap, other_edge_swap, 1, 1 - core),
        ):
            block = (half + dh) % 2 * 2 + owner
            group.append((source.at[:, :, frames], x.at[:, 0:4, frames, block]))
            group.append((ends.at[:, :, frames], x.at[:, 4:6, frames, block]))
        if tap is not None:
            taps = pl.ds(3 * tap, 3)
            for dz, source in ((0, w0), (1, w1), (3, w3)):
                group.append((source.at[taps], w.at[:, tap, :, (z + 4 - dz) % 4]))
            for which, source in ((odd, near), (1 - odd, far)):
                columns = pl.ds(pl.multiple_of(which * 256, 256), 256)
                group.append((source.at[taps], w.at[:, tap, :, (z + 2) % 4, :, columns]))
        start = sum(len(g) for g in groups)
        groups.append([fetch(start + i, *pair) for i, pair in enumerate(group)])
    for group in groups[:2]:
        for copy in group:
            copy.start()
    moments[...] = jnp.zeros_like(moments)
    lane = lax.broadcasted_iota(jnp.int32, (128, 128), 1)
    inside = (lane >= 4) & (lane < 124)

    def finish(t, g, summed):
        for h in range(2):
            part = summed[:, h * 128 : (h + 1) * 128]
            value = pltpu.roll(part[0:128], 1, 1) + part[128:256] + pltpu.roll(part[256:384], 127, 1)
            value = (value + bias[...]).astype(BF16).astype(F32)
            kept = jnp.where(inside, value, 0.0)
            moments[0] += kept
            moments[1] += kept * kept
            turned[...] = value.T
            for r, strip in enumerate((strip0, strip1, strip2, strip3)):
                strip[g * 2 + h, t] = turned[pl.ds(3 + 30 * ((half * 2 + core) ^ r), 32), :].astype(BF16)

    for source in range(6):
        if source < 4:
            for copy in groups[source]:
                copy.wait()
            for copy in groups[source + 2] if source < 2 else ():
                copy.start()
        taps = range(max(0, source - 3), min(2, source) + 1)
        for g in range(2):
            summed = None
            for b in range(3):
                rows = [(4, 0, 1, 2, 3, 5)[b + g * 2 + h] for h in range(2)]
                rhs = jnp.concatenate([x[:, r, source].reshape(512, 128) for r in rows], axis=1)
                lhs = w[b, taps[0] : taps[-1] + 1].reshape(len(taps) * 384, 512)
                term = jnp.dot(lhs, rhs, preferred_element_type=F32)
                summed = term if summed is None else summed + term
            for i, a in enumerate(taps):
                t = source - a
                part = summed[i * 384 : i * 384 + 384]
                if a == 0:
                    acc[t, g] = part
                elif a == 1:
                    acc[t, g] += part
                else:
                    finish(t, g, acc[t, g] + part)
    lane, group = (lax.broadcasted_iota(jnp.int32, (8, 128), i) for i in (1, 0))
    row = jnp.zeros((1, 128), F32)
    for i in range(2):
        grouped = jnp.sum(moments[i].reshape(8, 16, 128), axis=1)
        totals = jnp.sum(grouped, axis=1, keepdims=True)
        row += jnp.sum(jnp.where(lane == group + 8 * i, totals, 0.0), axis=0, keepdims=True)
    stats[...] = jnp.broadcast_to(row, (128, 128))


def conv_in(place, parts, weights, bias):
    return pl.pallas_call(
        conv_in_kernel,
        out_shape=[jax.ShapeDtypeStruct((4, 4, 32, 128), BF16)] * 4 + [jax.ShapeDtypeStruct((128, 128), F32)],
        in_specs=[pl.BlockSpec(memory_space=pltpu.SMEM)] + [pl.BlockSpec(memory_space=pl.ANY)] * 13
        + [pl.BlockSpec(memory_space=pltpu.VMEM)],
        out_specs=[pl.BlockSpec(memory_space=pltpu.VMEM)] * 5,
        scratch_shapes=[
            pltpu.VMEM((4, 6, 6, 4, 32, 128), BF16),
            pltpu.VMEM((3, 3, 3, 4, 32, 512), BF16),
            pltpu.VMEM((4, 2, 384, 256), F32),
            pltpu.VMEM((128, 128), F32),
            pltpu.VMEM((2, 128, 128), F32),
            pltpu.SemaphoreType.DMA((47,)),
        ],
        compiler_params=pltpu.CompilerParams(vmem_limit_bytes=56 * 1024 * 1024),
        cost_estimate=pl.CostEstimate(flops=7_200_000_000, bytes_accessed=9_000_000, transcendentals=0),
        name="conv_in",
    )(place, *parts, *weights, bias)


def collapse(taps, out):
    def pairs(t0, t1, t2):
        return ((t0, t1 + t2), (t0 + t1, t2))

    for z in range(4):
        for p in range(4):
            source = z * 128 + p * 32
            target = p * 128 + z * 32
            wide = [[taps[b, c, source : source + 32, :].astype(F32) for c in range(3)] for b in range(3)]
            by_col = [pairs(*row) for row in wide]
            for pw in range(2):
                for side in range(2):
                    by_row = pairs(by_col[0][pw][side], by_col[1][pw][side], by_col[2][pw][side])
                    for ph in range(2):
                        for j in range(2):
                            out[ph, j, pw, side * 512 + target : side * 512 + target + 32, :] = by_row[ph][j].astype(BF16)


def rim_kernel(rim, above, below, before, after, weight, out, w, wide, fine, sem):
    fetch = pltpu.make_async_copy(weight.at[0:2], w, sem)
    fetch.start()
    column = lax.broadcasted_iota(jnp.int32, (64, 512), 0)
    for t in range(2):
        for h in range(10):
            line = above[t] if h == 0 else below[t] if h == 9 else rim[t, h - 1]
            line = pltpu.roll(line.astype(F32), 1, 0)
            line = jnp.where(column == 0, before[t, h : h + 1].astype(F32), line)
            line = jnp.where(column == 61, after[t, h : h + 1].astype(F32), line)
            for s in range(3):
                moved = line if s == 0 else pltpu.roll(line, 64 - s, 0)
                wide[t, h, :, s * 512 : s * 512 + 512] = moved.astype(BF16)
    fetch.wait()
    for t in range(2):
        summed = None
        for a in range(2 - t):
            for b in range(3):
                lhs = wide[t + a, b : b + 8].reshape(512, 1536)
                term = jnp.dot(lhs, w[a, b], preferred_element_type=F32)
                summed = term if summed is None else summed + term
        for c in range(2):
            fine[...] = summed[:, c * 128 : c * 128 + 128].reshape(8, 64, 128)
            for r in range(8):
                for pw in range(2):
                    out[pw, r % 2, t, r // 2, :, c * 128 : c * 128 + 128] = fine[r, pl.ds(pw, 32, stride=2), :]


def conv_rim(rim, above, below, before, after, weight):
    return pl.pallas_call(
        rim_kernel,
        out_shape=jax.ShapeDtypeStruct((2, 2, 2, 4, 32, 256), F32),
        in_specs=[pl.BlockSpec(memory_space=pltpu.VMEM)] * 5 + [pl.BlockSpec(memory_space=pltpu.HBM)],
        out_specs=pl.BlockSpec(memory_space=pltpu.VMEM),
        scratch_shapes=[
            pltpu.VMEM((2, 3, 1536, 256), BF16),
            pltpu.VMEM((2, 10, 64, 1536), BF16),
            pltpu.VMEM((8, 64, 128), F32),
            pltpu.SemaphoreType.DMA,
        ],
        compiler_params=pltpu.CompilerParams(vmem_limit_bytes=50 * 1024 * 1024),
        cost_estimate=pl.CostEstimate(flops=7_200_000_000, bytes_accessed=8_000_000, transcendentals=0),
        name="conv_rim",
    )(rim, above, below, before, after, weight.reshape(3, 3, 1536, 256))


def conv_out_kernel(place, main, up, down, vectors, rim, bias, weight, out, n, acc, raw, w0, w1, w2, sems):
    fetches = [pltpu.make_async_copy(weight.at[tap], raw.at[tap], sems.at[tap]) for tap in range(3)]
    rim_fetch = pltpu.make_async_copy(rim, acc.at[:, :, 0:2], sems.at[3])
    for fetch in (*fetches, rim_fetch):
        fetch.start()
    own, left, right, top, bottom = (place[i] for i in range(5))
    row = lax.broadcasted_iota(jnp.int32, (32, 128), 0)
    keep_col = jnp.where(
        ((row == 0) & (left == 1)) | ((row == 31) & (right == 1)), 0.0, 1.0)
    keep = [keep_col] * 6
    keep[0] = keep_col * jnp.where(top == 1, 0.0, 1.0)
    keep[5] = keep_col * jnp.where(bottom == 1, 0.0, 1.0)

    def frame(t, _):
        for r in range(4):
            p = own ^ r
            vec = vectors[p]
            for h in range(6):
                raw = up[r, t] if h == 0 else down[r, t] if h == 5 else main[r, h - 1, t]
                v = (raw.astype(F32) - vec[0:1]) * vec[1:2] + vec[2:3]
                v = v / (1.0 + jnp.exp(-v)) * keep[h]
                for s in range(3):
                    moved = v if s == 0 else pltpu.roll(v, 32 - s, 0)
                    start = pl.multiple_of(s * 512 + p * 128, 128)
                    n[t, h, :, pl.ds(start, 128)] = moved.astype(BF16)
        return 0

    lax.fori_loop(0, 4, frame, 0)
    def multiply(tap, w):
        frames = 2 + tap
        for ph in range(2):
            for j in range(2):
                for pw in range(2):
                    lhs = n[0:frames, ph + j : ph + j + 4, :, pw * 512 : pw * 512 + 1024]
                    term = jnp.dot(lhs.reshape(frames * 128, 1024), w[ph, j, pw], preferred_element_type=F32)
                    term = term.reshape(frames, 4, 32, 256)
                    if tap == 2 and j == 0:
                        acc[pw, ph, 0:2] += term[0:2]
                        acc[pw, ph, 2:4] = term[2:4]
                    else:
                        acc[pw, ph, 4 - frames : 4] += term

    for fetch in (*fetches, rim_fetch):
        fetch.wait()
    collapse(raw.at[2], w2)
    multiply(2, w2)
    collapse(raw.at[1], w1)
    multiply(1, w1)
    collapse(raw.at[0], w0)
    multiply(0, w0)
    for pw in range(2):
        for t in range(4):
            rows = jnp.concatenate([acc[pw, r % 2, t, r // 2][None] for r in range(8)])
            out[:, pw, t] = (jnp.swapaxes(rows, 0, 1)[:30] + bias[...]).astype(BF16)


def conv_out(place, main, up, down, vectors, rim, bias, weight):
    whole = pl.BlockSpec(memory_space=pltpu.VMEM)
    return pl.pallas_call(
        conv_out_kernel,
        out_shape=jax.ShapeDtypeStruct((30, 2, 4, 8, 256), BF16),
        in_specs=[pl.BlockSpec(memory_space=pltpu.SMEM)] + [whole] * 4 + [pl.BlockSpec(memory_space=pl.ANY), whole, pl.BlockSpec(memory_space=pltpu.HBM)],
        out_specs=whole,
        scratch_shapes=[
            pltpu.VMEM((4, 6, 32, 1536), BF16),
            pltpu.VMEM((2, 2, 4, 4, 32, 256), F32),
            pltpu.VMEM((3, 3, 3, 512, 256), BF16),
            pltpu.VMEM((2, 2, 2, 1024, 256), BF16),
            pltpu.VMEM((2, 2, 2, 1024, 256), BF16),
            pltpu.VMEM((2, 2, 2, 1024, 256), BF16),
            pltpu.SemaphoreType.DMA((4,)),
        ],
        compiler_params=pltpu.CompilerParams(vmem_limit_bytes=52 * 1024 * 1024),
        cost_estimate=pl.CostEstimate(flops=4_900_000_000, bytes_accessed=18_000_000, transcendentals=400_000),
        name="conv_out",
    )(place, main, up, down, vectors, rim, bias, weight)


def body(
    latents,
    conv_in_weight,
    conv_in_bias,
    norm_gain,
    norm_shift,
    hidden_rim,
    conv_out_weight,
    conv_out_bias,
):
    chan, row = lax.axis_index("chan"), lax.axis_index("rows")
    z, half, core = chan // 4, chan // 2 % 2, chan % 2
    strip = chan % 4
    flip_core = lambda z, half, core, row: (z, half, 1 - core, row)

    flip_half = lambda z, half, core, row: (z, 1 - half, core, row)
    along_z = lambda dz: lambda z, half, core, row: (z + dz, half, core, row)

    weights = conv_in_weight.swapaxes(3, 4).reshape(9, 3, 32, 512)
    zones = [[c, c + 4, c + 8, c + 12] for c in range(4)]

    def to_zones(array):
        pieces = jnp.stack([array[..., 120 * i : 120 * i + 128] for i in range(4)])
        return lax.all_to_all(pieces, "chan", split_axis=0, concat_axis=0, axis_index_groups=zones, tiled=True)

    padded = jnp.pad(latents.transpose(2, 1, 3, 0), ((0, 0), (0, 0), (0, 0), (4, 28)))
    own = to_zones(padded)
    rim = jnp.pad(hidden_rim, ((0, 4), (0, 0), (0, 0), (0, 0))).transpose(1, 2, 0, 3)
    edge_rows = lambda i, j: jnp.concatenate([padded[i].reshape(192, 512), rim[:, j].reshape(128, 512)])
    above, below = send(edge_rows(3, 7), to_row(1)), send(edge_rows(0, 0), to_row(-1))
    odd = row % 2
    near = send(lax.dynamic_slice_in_dim(weights, odd * 256, 256, axis=3), along_z(2))
    own, weights = lax.optimization_barrier((own, weights))

    other = send(own, flip_half)
    w1, w3 = send(weights, along_z(1)), send(weights, along_z(3))
    far = send(near, lambda z, half, core, row: (z, half, core, row ^ 1))
    own_edge = to_zones(jnp.stack([above[:192].reshape(6, 32, 512), below[:192].reshape(6, 32, 512)]))
    other_edge = send(own_edge, flip_half)
    rim_above, rim_below = above[192:].reshape(2, 64, 512), below[192:].reshape(2, 64, 512)
    column = lambda i: jnp.concatenate([rim_above[:, None, i], rim[:, :, i], rim_below[:, None, i]], axis=1)
    before, after = send(column(59), to_chan(1)), send(column(0), to_chan(-1))
    other, before, after = lax.optimization_barrier((other, before, after))
    rim = conv_rim(rim, rim_above, rim_below, before, after, conv_out_weight)
    rim, own_late = lax.optimization_barrier((rim, own))
    own_swap = send(own_late, flip_core)
    other, other_edge, w1, w3, far, rim = lax.optimization_barrier((other, other_edge, w1, w3, far, rim))
    parts = [own, other, own_swap, send(other, flip_core),
             own_edge, other_edge, send(own_edge, flip_core), send(other_edge, flip_core)]
    weights = [weights, w1, w3, near, far]

    by_owner = conv_in_bias.reshape(4, 4, 32)
    bias = lax.dynamic_index_in_dim(by_owner, strip, 1, keepdims=False).reshape(128, 1)
    place = jnp.stack([z, half, core, odd]).astype(jnp.int32)
    *strips, stats = conv_in(place, parts, weights, jnp.broadcast_to(bias, (128, 128)))

    parts = strips[:1] + [
        send(strips[r], lambda z, half, core, row: (z, half ^ (r // 2), core ^ (r % 2), row)) for r in range(1, 4)]
    stats, parts[1] = lax.optimization_barrier((stats, parts[1]))
    first = jnp.stack(parts)
    above, below = send(first[:, 3], to_row(1)), send(first[:, 0], to_row(-1))
    gathered = lax.all_to_all(stats, BOTH, split_axis=0, concat_axis=0, tiled=True)
    sums, squares = gathered.reshape(4, 4, 8, 128)[..., :16].sum(axis=(0, 2)).reshape(4, 2, 8).swapaxes(0, 1)
    counted = float(480 * 4 * 32 * 16)
    mean = sums / counted
    var = squares / counted - mean * mean
    inv = 1.0 / jnp.sqrt(var + 1e-06)
    by_place = lambda vector: vector.reshape(4, 4, 32).swapaxes(0, 1).reshape(4, 128)
    vectors = jnp.stack(
        [jnp.repeat(mean, 16, axis=1), jnp.repeat(inv, 16, axis=1) * by_place(norm_gain), by_place(norm_shift)]
        + [jnp.zeros((4, 128), F32)] * 5, axis=1)
    edges = jnp.stack([strip, chan == 0, chan == 15, row == 0, row == 7]).astype(jnp.int32)
    decoded = conv_out(edges, first, above, below, vectors, rim, conv_out_bias.reshape(1, 256),
                       conv_out_weight)
    return decoded.reshape(60, 4, 8, 256)


def solution(mesh):
    return jax.shard_map(
        body,
        mesh=mesh,
        in_specs=(
            P(None, None, "rows", "chan"),
            P(None, None, None, None, "chan"),
            P(),
            P(),
            P(),
            P("chan", None, "rows", None),
            P(),
            P(),
        ),
        out_specs=P("chan", None, "rows", None),
        check_vma=False,
    )
```
